32 devices in a mesh: bricks: 4 (over y, x), grp: 8 (over z, core).
Axes of the slice: x: 2, y: 2, z: 4, core: 2. Of those that a mesh axis runs over, the one named last changes fastest.
Arguments:
- features: bfloat16 [256, 64, 512], P(('bricks', 'grp')), may hold values from -6 to 6
- occupancy: int32 [256, 512], P(('bricks', 'grp')), may hold values from 0 to 1
- neighbours: int32 [256, 26], P(('bricks', 'grp')), may hold values from -1 to 255, as said below
- coarse_map: int32 [256], P(('bricks', 'grp')), may hold values from 0 to 255, as said below
- norm_gain: float32 [64], replicated, may hold values from 0.1 to 1.9
- time_shift: float32 [64], replicated, may hold values from -4 to 4
- conv_weight: bfloat16 [27, 64, 64], replicated, may hold values from -0.15625 to 0.15625
- stride_weight: bfloat16 [8, 64, 128], replicated, may hold values from -0.25 to 0.25
- coarse_bias: float32 [128], replicated, may hold values from -3 to 3
Outputs:
- fine_out: bfloat16 [256, 64, 512], P(('bricks', 'grp'))
- coarse_out: bfloat16 [32, 128, 512], P(('bricks', 'grp'))
The draws below stay inside these ranges and needn't reach their ends.
Inputs may be any that keep to these rules, and one draw needn't show every extreme that they name: The key orders bricks by x-slab: brick i lies on device i // 8 of bricks+grp, in the slab of cells with x coordinate i // 8. neighbours[i, o] names the brick at offset o from brick i, or -1 where that cell holds no active brick or lies outside the grid. `coarse_map`: every coarse brick has all eight octants, each named once. Coarse brick c is held by device c // 1. Its eight children lie four on device 2 k and four on device 2 k + 1, with k = c // 2; so each device holds the coarse bricks of exactly 4 of its own bricks, and the coarse bricks of its other 4 bricks are held by the device whose index differs in the lowest bit.
All inputs are finite; a program needn't handle non-finite values.
Results may differ from the reference program's by a relative error of at most 0.0047.
Values may be sent and summed in bfloat16 or wider, within the bound.
A program may use at most 128 MiB of HBM per device.

```python
import jax
import jax.numpy as jnp
from jax import lax

C = 64
C2 = 128
VOX = 512
BRK_DEV = 8
NSLAB = 32
NBRICK = 256


def layout(key):
    quads = BRK_DEV // 2
    pairs = NSLAB // 2
    pair_keys = jax.random.split(jax.random.fold_in(key, 7), pairs)
    chosen = jax.vmap(lambda single: jax.random.permutation(single, quads))(pair_keys)[:, :BRK_DEV // 4]
    quad_on = jnp.zeros((pairs, quads), jnp.int32).at[jnp.arange(pairs)[:, None], chosen].set(1)
    cell_y = jnp.arange(2 * BRK_DEV) // 8
    cell_z = jnp.arange(2 * BRK_DEV) % 8
    cell_quad = cell_y // 2 * 4 + cell_z // 2
    cell_on = jnp.repeat(quad_on[:, cell_quad], 2, axis=0)
    cell_rank = jnp.cumsum(cell_on, axis=1) - 1
    cell_of = jax.vmap(lambda row: jnp.nonzero(row, size=BRK_DEV)[0])(cell_on).astype(jnp.int32)
    return (cell_on, cell_rank, cell_of, quad_on)


def draw_neighbours(key, part):
    cell_on, cell_rank, cell_of, quad_on = layout(key)
    slab = jnp.arange(NSLAB, dtype=jnp.int32)[:, None]
    pos_y = cell_of // 8
    pos_z = cell_of % 8
    extent_y = BRK_DEV // 4
    columns = []
    for shift_x in (-1, 0, 1):
        for shift_y in (-1, 0, 1):
            for shift_z in (-1, 0, 1):
                if shift_x == 0 and shift_y == 0 and (shift_z == 0):
                    continue
                target_x = slab + shift_x + 0 * pos_y
                target_y = pos_y + shift_y
                target_z = pos_z + shift_z
                inside = (target_x >= 0) & (target_x < NSLAB) & (target_y >= 0) & (target_y < extent_y) & (target_z >= 0) & (target_z < 8)
                clip_x = jnp.clip(target_x, 0, NSLAB - 1)
                clip_cell = jnp.clip(target_y, 0, extent_y - 1) * 8 + jnp.clip(target_z, 0, 7)
                present = cell_on[clip_x, clip_cell] == 1
                target = clip_x * BRK_DEV + cell_rank[clip_x, clip_cell]
                columns.append(jnp.where(inside & present, target, -1))
    return jnp.stack(columns, axis=-1).reshape(NSLAB * BRK_DEV, 26).astype(jnp.int32)


def draw_coarse_map(key, part):
    cell_on, cell_rank, cell_of, quad_on = layout(key)
    pairs = NSLAB // 2
    quad_rank = jnp.cumsum(quad_on, axis=1) - 1
    perm_keys = jax.random.split(jax.random.fold_in(key, 11), pairs)
    relabel = jax.vmap(lambda single: jax.random.permutation(single, BRK_DEV // 4))(perm_keys).astype(jnp.int32)
    slab = jnp.arange(NSLAB, dtype=jnp.int32)[:, None] + 0 * cell_of
    pos_y = cell_of // 8
    pos_z = cell_of % 8
    quad = pos_y // 2 * 4 + pos_z // 2
    ranked = quad_rank[slab // 2, quad]
    shuffled = relabel[slab // 2, ranked]
    coarse_id = slab // 2 * (BRK_DEV // 4) + shuffled
    octant = slab % 2 * 4 + pos_y % 2 * 2 + pos_z % 2
    return (coarse_id * 8 + octant).reshape(-1).astype(jnp.int32)


def draw_occupancy(key, part):
    total = NSLAB * BRK_DEV
    density = jax.random.randint(jax.random.fold_in(key, 3), (total, 1), 250, 900)
    rolled = jax.random.randint(jax.random.fold_in(key, 5), (total, VOX), 0, 1000)
    return (rolled < density).astype(jnp.int32)


def level_of(stream_key, dims, cuts, low, largest):
    factor_of = 1.0
    for axis_at, parts in cuts:
        heights = jax.random.uniform(jax.random.fold_in(jax.random.fold_in(stream_key, 6), axis_at), (parts,), jnp.float32, low / len(cuts), largest / len(cuts))
        factor_of = factor_of * jnp.repeat(jnp.exp(heights), dims[axis_at] // parts).reshape((-1,) + (1,) * (len(dims) - 1 - axis_at))
    return factor_of


def normal_values(own_key, shape, scale, bound, cuts=(), held_as=jnp.bfloat16):
    entries = scale * jax.random.normal(own_key, shape, jnp.float32)
    if cuts:
        entries = entries * level_of(own_key, shape, cuts, -0.22, 0.18)
    return jnp.clip(entries, -bound, bound).astype(held_as)


def setup_inputs(seed: int = 0) -> dict:
    splits = jax.random.split(jax.random.key(seed), 10)
    return {
        "features": normal_values(splits[0], (NBRICK, C, VOX), 1.0, 6.0, ((0, 32),)),
        "occupancy": draw_occupancy(jax.random.fold_in(splits[9], 71), 0),
        "neighbours": draw_neighbours(jax.random.fold_in(splits[9], 71), 0),
        "coarse_map": draw_coarse_map(jax.random.fold_in(splits[9], 71), 0),
        "norm_gain": jnp.clip(1.0 + 0.18 * jax.random.normal(splits[4], (C,), jnp.float32), 0.1, 1.9),
        "time_shift": normal_values(splits[5], (C,), 1.0, 4.0, (), jnp.float32),
        "conv_weight": normal_values(splits[6], (27, C, C), (27 * C) ** -0.5, 0.15625),
        "stride_weight": normal_values(splits[7], (8, C, C2), (8 * C) ** -0.5, 0.25),
        "coarse_bias": normal_values(splits[8], (C2,), 0.5, 3.0, (), jnp.float32),
    }


norm_eps = 1e-06

def activate(features, occupancy, norm_gain):
    values = features.astype(jnp.float32)
    scale = lax.rsqrt(lax.optimization_barrier(jnp.mean(values * values, axis=1, keepdims=True)) + norm_eps)
    normed = values * scale * norm_gain[None, :, None]
    mask = occupancy[:, None, :].astype(jnp.float32)
    return (jax.nn.silu(normed) * mask).astype(jnp.bfloat16)

def layer_slice(cubes, axis_pos, shift):
    if shift == -1:
        return lax.slice_in_dim(cubes, 7, 8, axis=axis_pos)
    if shift == 1:
        return lax.slice_in_dim(cubes, 0, 1, axis=axis_pos)
    return cubes

def assemble(center, fetch):
    bricks_here = center.shape[0]
    channels = center.shape[1]
    cube = center.reshape(bricks_here, channels, 8, 8, 8)
    planes = []
    position = 0
    for shift_x in (-1, 0, 1):
        rows_y = []
        for shift_y in (-1, 0, 1):
            cols_z = []
            for shift_z in (-1, 0, 1):
                if shift_x == 0 and shift_y == 0 and (shift_z == 0):
                    cols_z.append(cube)
                else:
                    cols_z.append(fetch(position, shift_x, shift_y, shift_z))
                    position += 1
            rows_y.append(jnp.concatenate(cols_z, axis=4))
        planes.append(jnp.concatenate(rows_y, axis=3))
    return jnp.concatenate(planes, axis=2)

def convolve(padded, conv_weight):
    bricks_here = padded.shape[0]
    channels = padded.shape[1]
    total = jnp.zeros((bricks_here, conv_weight.shape[2], 512), jnp.float32)
    for start_x in range(3):
        for start_y in range(3):
            taps = []
            for start_z in range(3):
                window = padded[:, :, start_x:start_x + 8, start_y:start_y + 8, start_z:start_z + 8]
                taps.append(window.reshape(bricks_here, channels, 512))
            stacked = jnp.concatenate(taps, axis=1).astype(jnp.float32)
            first_tap = 9 * start_x + 3 * start_y
            weight = conv_weight[first_tap:first_tap + 3].reshape(3 * channels, -1).astype(jnp.float32)
            total = total + jnp.einsum('bcp,cd->bdp', stacked, weight)
    return total

def reduce_resolution(fine_features, stride_weight, coarse_bias):
    bricks_here = fine_features.shape[0]
    channels = fine_features.shape[1]
    split = fine_features.reshape(bricks_here, channels, 4, 2, 4, 2, 4, 2).astype(jnp.float32)
    kernel = stride_weight.reshape(2, 2, 2, channels, -1).astype(jnp.float32)
    octant = jnp.einsum('nciajbkd,abdce->neijk', split, kernel)
    octant = octant + coarse_bias[None, :, None, None, None]
    return octant.reshape(bricks_here, -1).astype(jnp.bfloat16)

def assemble_coarse(placed, coarse_count):
    wide = placed.shape[1] // 64
    shaped = placed.reshape(coarse_count, 2, 2, 2, wide, 4, 4, 4)
    return shaped.transpose(0, 4, 1, 5, 2, 6, 3, 7).reshape(coarse_count, wide, 512)

def reference(features, occupancy, neighbours, coarse_map, norm_gain, time_shift, conv_weight, stride_weight, coarse_bias):
    total_bricks = features.shape[0]
    channels = features.shape[1]
    active = activate(features, occupancy, norm_gain)
    cubes = active.reshape(total_bricks, channels, 8, 8, 8)
    block = 256 if total_bricks % 256 == 0 else total_bricks

    def one_block(number):
        start = (number * block).astype(jnp.int32)
        centre = lax.dynamic_slice_in_dim(active, start, block, 0)
        listed = lax.dynamic_slice_in_dim(neighbours, start, block, 0)
        raw = lax.dynamic_slice_in_dim(features, start, block, 0)
        mask = lax.dynamic_slice_in_dim(occupancy, start, block, 0)

        def fetch(position, shift_x, shift_y, shift_z):
            target = listed[:, position]
            rows = jnp.take(cubes, jnp.maximum(target, 0).astype(jnp.int32), axis=0)
            piece = layer_slice(layer_slice(layer_slice(rows, 2, shift_x), 3, shift_y), 4, shift_z)
            keep = (target >= 0).astype(piece.dtype)
            return piece * keep[:, None, None, None, None]
        padded = assemble(centre, fetch)
        conv = convolve(padded, conv_weight)
        summed = raw.astype(jnp.float32) + conv + time_shift[None, :, None]
        hidden_state = (mask[:, None, :].astype(jnp.float32) * summed).astype(jnp.bfloat16)
        return (hidden_state, reduce_resolution(hidden_state, stride_weight, coarse_bias))
    hidden_state, octant_list = lax.map(one_block, jnp.arange(total_bricks // block, dtype=jnp.int32))
    hidden_state = hidden_state.reshape(total_bricks, channels, 512)
    octant_list = octant_list.reshape(total_bricks, -1)
    placed = jnp.zeros_like(octant_list).at[coarse_map.astype(jnp.int32)].set(octant_list)
    return (hidden_state, assemble_coarse(placed, total_bricks // 8))
```

```python
import functools

import jax
import jax.numpy as jnp
import numpy as np
from jax import lax
from jax.experimental import pallas as pl
from jax.experimental.pallas import tpu as pltpu
from jax.sharding import PartitionSpec as P

norm_eps = 1e-06
AXES = ("bricks", "grp")
SHIFTS = [(b, c) for b in (-1, 0, 1) for c in (-1, 0, 1)]


def window_matrix():
    table = np.zeros((4, 2, 64, 9, 2, 64), np.float32)
    for w, (b, c) in enumerate(SHIFTS):
        for y in range(8):
            for z in range(8):
                yy, zz = y + b, z + c
                kind = (1 if not 0 <= yy < 8 else 0) + (2 if not 0 <= zz < 8 else 0)
                for half in range(2):
                    table[kind, half, (yy % 8) * 8 + zz % 8, w, half, y * 8 + z] = 1.0
    return table.reshape(512, 1152).astype(jnp.bfloat16)


def stride_matrix():
    table = np.zeros((512, 512), np.float32)
    for x in range(8):
        for y in range(8):
            for z in range(8):
                tap = 4 * (x % 2) + 2 * (y % 2) + z % 2
                place = 16 * (x // 2) + 4 * (y // 2) + z // 2
                table[64 * x + 8 * y + z, 64 * tap + place] = 1.0
    return table.astype(jnp.bfloat16)


def activate(features, occupancy, norm_gain):
    values = features.astype(jnp.float32)
    scale = lax.rsqrt(jnp.mean(values * values, axis=1, keepdims=True) + norm_eps)
    normed = values * scale * norm_gain[None, :, None]
    mask = occupancy[:, None, :].astype(jnp.float32)
    return (jax.nn.silu(normed) * mask).astype(jnp.bfloat16)


def column(row):
    n = row.shape[1]
    at = lax.broadcasted_iota(jnp.int32, (n, n), 0)
    to = lax.broadcasted_iota(jnp.int32, (n, n), 1)
    return jnp.sum(jnp.where(at == to, row, 0.0), axis=1, keepdims=True)


def offset(dx, dy, dz):
    o = 9 * (dx + 1) + 3 * (dy + 1) + dz + 1
    return o - 1 if o > 13 else o


def dot(a, b):
    return jnp.dot(a, b, preferred_element_type=jnp.float32)


def halos(fetch, masks):
    low_y, low_z = masks
    high_y, high_z = 1 - low_y, 1 - low_z
    halo_y = fetch(1, 0) * low_y + fetch(-1, 0) * high_y
    halo_z = fetch(0, 1) * low_z + fetch(0, -1) * high_z
    near = fetch(1, 1) * low_z + fetch(1, -1) * high_z
    far = fetch(-1, 1) * low_z + fetch(-1, -1) * high_z
    return halo_y, halo_z, near * low_y + far * high_y


def fine_kernel(
    near_ref, feat_ref, occ_ref, before_ref, after_ref, gain_ref, shift_ref, bias_ref,
    weight_ref, stride_ref, window_ref, perm_ref,
    fine_ref, oct_ref,
    act, lower, upper,
):
    count = feat_ref.shape[0]
    device = lax.axis_index("bricks") * lax.axis_size("grp") + lax.axis_index("grp")
    gain = column(gain_ref[...])
    shift = column(shift_ref[...])
    bias = column(bias_ref[...])

    def activate_one(i, carry):
        values = feat_ref[i].astype(jnp.float32)
        scale = lax.rsqrt(jnp.mean(values * values, axis=0, keepdims=True) + norm_eps)
        normed = values * scale * gain
        mask = occ_ref[pl.ds(i, 1), :].astype(jnp.float32)
        act[i] = (normed / (1.0 + jnp.exp(-normed)) * mask).astype(jnp.bfloat16)
        return carry

    lax.fori_loop(0, count, activate_one, 0)
    act[count] = jnp.zeros((64, 512), jnp.bfloat16)
    lower[0:count] = before_ref[...]
    upper[0:count] = after_ref[...]
    lower[count] = jnp.zeros((64, 128), jnp.bfloat16)
    upper[count] = jnp.zeros((64, 128), jnp.bfloat16)

    lane = lax.broadcasted_iota(jnp.int32, (64, 512), 1)
    low_y = jnp.where(lane % 64 < 32, 1.0, 0.0).astype(jnp.bfloat16)
    low_z = jnp.where(lane % 8 < 4, 1.0, 0.0).astype(jnp.bfloat16)
    half = lax.broadcasted_iota(jnp.int32, (64, 128), 1) < 64
    first = jnp.where(half, 1.0, 0.0).astype(jnp.bfloat16)
    second = 1 - first

    def brick(i, carry):
        def row(dx, dy, dz):
            target = near_ref[i, offset(dx, dy, dz)]
            local = jnp.clip(target - (device + dx) * count, 0, count - 1)
            return jnp.where(target < 0, count, local)

        def own(dy, dz):
            return act[row(0, dy, dz)]

        def outer(dy, dz):
            return upper[row(1, dy, dz)] * first + lower[row(-1, dy, dz)] * second

        middle = (act[i],) + halos(own, (low_y, low_z))
        edge = (outer(0, 0),) + halos(outer, (low_y[:, :128], low_z[:, :128]))
        rows = [
            jnp.concatenate([m[:, 128 * p : 128 * p + 128] for m in middle], axis=1)
            for p in range(4)
        ]
        rows.append(jnp.concatenate(edge, axis=1))
        windows = dot(jnp.concatenate(rows, axis=0), window_ref[...]).astype(jnp.bfloat16)
        stacked = jnp.concatenate(
            [
                jnp.concatenate(
                    [windows[64 * p : 64 * p + 64, 128 * w : 128 * w + 128] for w in range(9)],
                    axis=0,
                )
                for p in range(5)
            ],
            axis=1,
        )
        product = dot(weight_ref[...], stacked)

        def part(dx, p):
            p = p % 5
            return product[64 * (dx + 1) : 64 * (dx + 2), 128 * p : 128 * p + 128]

        pieces = []
        for p in range(4):
            below = pltpu.roll(jnp.where(half, part(-1, p), part(-1, p - 1)), 64, 1)
            above = pltpu.roll(jnp.where(half, part(1, p + 1), part(1, p)), 64, 1)
            pieces.append(part(0, p) + below + above)
        conv = jnp.concatenate(pieces, axis=1)
        mask = occ_ref[pl.ds(i, 1), :].astype(jnp.float32)
        summed = feat_ref[i].astype(jnp.float32) + conv + shift
        fine_ref[i] = (mask * summed).astype(jnp.bfloat16)
        return carry

    lax.fori_loop(0, count, brick, 0)

    sorted_ = dot(fine_ref[...].reshape(count * 64, 512), perm_ref[...])
    columns = []
    for j in range(0, count, 2):
        taps = []
        for s in range(4):
            one = sorted_[64 * j : 64 * j + 64, 128 * s : 128 * s + 128]
            two = sorted_[64 * j + 64 : 64 * j + 128, 128 * s : 128 * s + 128]
            taps.append(jnp.where(half, one, pltpu.roll(two, 64, 1)))
            taps.append(jnp.where(half, pltpu.roll(one, 64, 1), two))
        columns.append(jnp.concatenate(taps, axis=0).astype(jnp.bfloat16))
    octants = dot(stride_ref[...], jnp.concatenate(columns, axis=1)) + bias
    oct_ref[...] = octants.astype(jnp.bfloat16)


def place(map_ref, octants, coarse, count):
    k = lax.broadcasted_iota(jnp.int32, (64, 512), 0)
    lane = lax.broadcasted_iota(jnp.int32, (64, 512), 1)
    rest = lane - (64 * (k // 16) + 8 * (k // 4 % 4) + k % 4)
    blocks = []
    for j in range(count):
        key = map_ref[j]
        o = key % 8
        start = 256 * (o // 4) + 32 * (o // 2 % 2) + 4 * (o % 2)
        start = jnp.where(key // 8 == coarse, start, -1024)
        blocks.append(jnp.where(rest == start, 1.0, 0.0).astype(jnp.bfloat16))
    return dot(octants, jnp.concatenate(blocks, axis=0))


def coarse_kernel(map_ref, other_ref, oct_ref, came_ref, out_ref):
    count = map_ref.shape[0]
    device = lax.axis_index("bricks") * lax.axis_size("grp") + lax.axis_index("grp")
    total = place(map_ref, oct_ref[...], device, count)
    total = total + place(other_ref, came_ref[...], device, count)
    out_ref[0] = total.astype(jnp.bfloat16)


def partner(x):
    return lax.ppermute(x, "grp", [(i, i ^ 1) for i in range(lax.axis_size("grp"))])


def shards(
    features, occupancy, neighbours, coarse_map, norm_gain, time_shift, conv_weight,
    stride_weight, coarse_bias,
):
    count = features.shape[0]
    peers = lax.axis_size(AXES)
    up = [(i, i + 1) for i in range(peers - 1)]
    down = [(j, i) for i, j in up]
    last = activate(features[:, :, 384:], occupancy[:, 384:], norm_gain)
    first = activate(features[:, :, :128], occupancy[:, :128], norm_gain)
    before = lax.ppermute(last, AXES, up)
    after = lax.ppermute(first, AXES, down)
    other_map = partner(coarse_map)
    weight = conv_weight.reshape(3, 576, 64).transpose(0, 2, 1).reshape(192, 576)
    stride = stride_weight.reshape(512, 128).T
    vmem = pl.BlockSpec(memory_space=pltpu.VMEM)
    smem = pl.BlockSpec(memory_space=pltpu.SMEM)
    params = pltpu.CompilerParams(vmem_limit_bytes=48 * 1024 * 1024)
    fine, octants = pl.pallas_call(
        fine_kernel,
        out_shape=(
            jax.ShapeDtypeStruct(features.shape, jnp.bfloat16),
            jax.ShapeDtypeStruct((128, 64 * count), jnp.bfloat16),
        ),
        in_specs=[smem] + [vmem] * 11,
        out_specs=(vmem, vmem),
        scratch_shapes=[
            pltpu.VMEM((count + 1, 64, 512), jnp.bfloat16),
            pltpu.VMEM((count + 1, 64, 128), jnp.bfloat16),
            pltpu.VMEM((count + 1, 64, 128), jnp.bfloat16),
        ],
        compiler_params=params,
        name="fine",
    )(
        neighbours, features, occupancy, before, after, norm_gain[None], time_shift[None],
        coarse_bias[None], weight, stride, window_matrix(), stride_matrix(),
    )
    came = partner(octants)
    coarse = pl.pallas_call(
        coarse_kernel,
        out_shape=jax.ShapeDtypeStruct((1, 128, 512), jnp.bfloat16),
        in_specs=[smem, smem, vmem, vmem],
        out_specs=vmem,
        compiler_params=params,
        name="coarse",
    )(coarse_map, other_map, octants, came)
    return fine, coarse


def solution(mesh):
    wide = P(AXES, None, None)
    return jax.shard_map(
        shards,
        mesh=mesh,
        in_specs=(wide, P(AXES, None), P(AXES, None), P(AXES), P(), P(), P(), P(), P()),
        out_specs=(wide, wide),
        check_vma=False,
    )
```

```python
import jax
import jax.numpy as jnp
import numpy as np
from jax import lax
from jax.experimental import pallas as pl
from jax.experimental.pallas import tpu as pltpu
from jax.sharding import PartitionSpec as P

norm_eps = 1e-06
AXES = ("bricks", "grp")


def window_matrix(shifts, kinds):
    table = np.zeros((4, 2, 64, len(shifts), 2, 64), np.float32)
    for w, (b, c) in enumerate(shifts):
        for y in range(8):
            for z in range(8):
                yy, zz = y + b, z + c
                kind = (1 if not 0 <= yy < 8 else 0) + (2 if not 0 <= zz < 8 else 0)
                for half in range(2):
                    table[kind, half, (yy % 8) * 8 + zz % 8, w, half, y * 8 + z] = 1.0
    return table[kinds].reshape(128 * len(kinds), 128 * len(shifts)).astype(jnp.bfloat16)


def stride_matrix():
    table = np.zeros((512, 512), np.float32)
    for x in range(8):
        for y in range(8):
            for z in range(8):
                tap = 4 * (x % 2) + 2 * (y % 2) + z % 2
                place = 16 * (x // 2) + 4 * (y // 2) + z // 2
                table[64 * x + 8 * y + z, 64 * tap + place] = 1.0
    return table.astype(jnp.bfloat16)


def column(row):
    n = row.shape[1]
    at = lax.broadcasted_iota(jnp.int32, (n, n), 0)
    to = lax.broadcasted_iota(jnp.int32, (n, n), 1)
    return jnp.sum(jnp.where(at == to, row, 0.0), axis=1, keepdims=True)


def offset(dx, dy, dz):
    o = 9 * (dx + 1) + 3 * (dy + 1) + dz + 1
    return o - 1 if o > 13 else o


def dot(a, b):
    return jnp.dot(a, b, preferred_element_type=jnp.float32)


def halos(fetch, masks):
    low_y, low_z = masks
    high_y, high_z = 1 - low_y, 1 - low_z
    halo_y = fetch(1, 0) * low_y + fetch(-1, 0) * high_y
    halo_z = fetch(0, 1) * low_z + fetch(0, -1) * high_z
    near = fetch(1, 1) * low_z + fetch(1, -1) * high_z
    far = fetch(-1, 1) * low_z + fetch(-1, -1) * high_z
    return halo_y, halo_z, near * low_y + far * high_y


def flipped(x):
    n = x.shape[1]
    at = lax.broadcasted_iota(jnp.int32, (n, n), 0)
    to = lax.broadcasted_iota(jnp.int32, (n, n), 1)
    eye = jnp.where(at == to, 1.0, 0.0).astype(jnp.bfloat16)
    dims = (((1,), (1,)), ((), ()))
    return lax.dot_general(eye, x, dims, preferred_element_type=jnp.float32).astype(jnp.bfloat16)


def stack(centre, halo_y, halo_z, corner, side_y, side_z, side_yz):
    tiles = centre.shape[0] // 64
    pair_y = dot(jnp.concatenate([centre, halo_y], axis=1), side_y).astype(jnp.bfloat16)
    pair_z = dot(jnp.concatenate([centre, halo_z], axis=1), side_z).astype(jnp.bfloat16)
    four = jnp.concatenate([centre, halo_y, halo_z, corner], axis=1)
    quad = dot(four, side_yz).astype(jnp.bfloat16)
    order = [
        (quad, 0), (pair_y, 0), (quad, 1), (pair_z, 0), (centre, 0),
        (pair_z, 1), (quad, 2), (pair_y, 1), (quad, 3),
    ]
    return jnp.concatenate(
        [
            jnp.concatenate(
                [m[64 * p : 64 * p + 64, 128 * w : 128 * w + 128] for m, w in order], axis=0
            )
            for p in range(tiles)
        ],
        axis=1,
    )


def place(keys, octants, coarse, count):
    k = lax.broadcasted_iota(jnp.int32, (64, 512), 0)
    lane = lax.broadcasted_iota(jnp.int32, (64, 512), 1)
    rest = lane - (64 * (k >> 4) + 8 * ((k >> 2) & 3) + (k & 3))
    o = keys & 7
    starts = 256 * (o >> 2) + 32 * ((o >> 1) & 1) + 4 * (o & 1)
    starts = jnp.where((keys >> 3) == coarse, starts, -1024)
    starts = jnp.concatenate([starts] * 4, axis=1)
    blocks = [
        jnp.where(rest == starts[j : j + 1], 1.0, 0.0).astype(jnp.bfloat16) for j in range(count)
    ]
    return dot(octants, jnp.concatenate(blocks, axis=0))


def kernel(
    near_ref, occ_ref, map_ref, gain_ref, shift_ref, bias_ref,
    feat_hbm, weight_hbm, stride_hbm, side_y_hbm, side_z_hbm, side_yz_hbm, perm_hbm,
    fine_hbm, coarse_ref,
    feat, weight, stride, side_y, side_z, side_yz, perm,
    act, lower, upper, conv, fine, weight_t, keys, keys_in, octs, octs_in,
    local_sem, send_sem, recv_sem,
):
    count = feat.shape[0]
    groups = lax.axis_size("grp")
    peers = groups * lax.axis_size("bricks")
    device = lax.axis_index("bricks") * groups + lax.axis_index("grp")
    has_left = device > 0
    has_right = device < peers - 1

    def coords(other):
        return {"bricks": other // groups, "grp": other % groups}

    loads = [
        pltpu.make_async_copy(src, dst, local_sem.at[n])
        for n, (src, dst) in enumerate(
            [
                (feat_hbm, feat), (weight_hbm, weight), (side_y_hbm, side_y),
                (side_z_hbm, side_z), (side_yz_hbm, side_yz), (perm_hbm, perm),
                (stride_hbm, stride),
            ]
        )
    ]
    for load in loads:
        load.start()
    barrier = pltpu.get_barrier_semaphore()

    @pl.when(has_left)
    def _():
        pl.semaphore_signal(
            barrier, inc=1, device_id=coords(device - 1), device_id_type=pl.DeviceIdType.MESH
        )

    @pl.when(has_right)
    def _():
        pl.semaphore_signal(
            barrier, inc=1, device_id=coords(device + 1), device_id_type=pl.DeviceIdType.MESH
        )

    gain = column(gain_ref[...])
    shift = column(shift_ref[...])
    bias = column(bias_ref[...])
    keys[...] = jnp.broadcast_to(
        column(map_ref[...].astype(jnp.float32)).astype(jnp.int32), keys.shape
    )
    act[count] = jnp.zeros((64, 512), jnp.bfloat16)
    lower[count] = jnp.zeros((64, 128), jnp.bfloat16)
    upper[count] = jnp.zeros((64, 128), jnp.bfloat16)

    @pl.when(jnp.logical_not(has_left))
    def _():
        lower[0:count] = jnp.zeros((count, 64, 128), jnp.bfloat16)

    @pl.when(jnp.logical_not(has_right))
    def _():
        upper[0:count] = jnp.zeros((count, 64, 128), jnp.bfloat16)

    loads[0].wait()

    def activate_one(i, carry):
        values = feat[i].astype(jnp.float32)
        scale = lax.rsqrt(jnp.mean(values * values, axis=0, keepdims=True) + norm_eps)
        normed = values * scale * gain
        mask = occ_ref[pl.ds(i, 1), :].astype(jnp.float32)
        act[i] = (normed / (1.0 + jnp.exp(-normed)) * mask).astype(jnp.bfloat16)
        return carry

    lax.fori_loop(0, count, activate_one, 0)

    def remote(n, src, dst, other):
        return pltpu.make_async_remote_copy(
            src_ref=src, dst_ref=dst, send_sem=send_sem.at[n], recv_sem=recv_sem.at[n],
            device_id=coords(other), device_id_type=pl.DeviceIdType.MESH,
        )

    bricks = pl.ds(0, count)
    rise = remote(0, act.at[bricks, :, pl.ds(384, 128)], lower.at[bricks], device + 1)
    fall = remote(1, act.at[bricks, :, pl.ds(0, 128)], upper.at[bricks], device - 1)
    mate = device + 1 - 2 * (device % 2)
    swap_keys = remote(2, keys, keys_in, mate)
    swap_octs = remote(3, octs, octs_in, mate)

    pl.semaphore_wait(barrier, has_left.astype(jnp.int32) + has_right.astype(jnp.int32))

    @pl.when(has_right)
    def _():
        rise.start()

    @pl.when(has_left)
    def _():
        fall.start()

    swap_keys.start()

    for load in loads[1:]:
        load.wait()
    for a in range(3):
        weight_t[64 * a : 64 * a + 64] = flipped(weight[576 * a : 576 * a + 576])

    lane = lax.broadcasted_iota(jnp.int32, (64, 512), 1)
    low_y = jnp.where(lane % 64 < 32, 1.0, 0.0).astype(jnp.bfloat16)
    low_z = jnp.where(lane % 8 < 4, 1.0, 0.0).astype(jnp.bfloat16)
    half = lax.broadcasted_iota(jnp.int32, (64, 128), 1) < 64
    first = jnp.where(half, 1.0, 0.0).astype(jnp.bfloat16)
    second = 1 - first

    def row(i, dx, dy, dz):
        target = near_ref[i, offset(dx, dy, dz)]
        local = jnp.clip(target - (device + dx) * count, 0, count - 1)
        return jnp.where(target < 0, count, local)

    def middle(i, carry):
        def own(dy, dz):
            return act[row(i, 0, dy, dz)]

        wide = (act[i],) + halos(own, (low_y, low_z))
        tall = [
            jnp.concatenate([m[:, 128 * p : 128 * p + 128] for p in range(4)], axis=0)
            for m in wide
        ]
        stacked = stack(*tall, side_y[...], side_z[...], side_yz[...])
        product = dot(weight_t[...], stacked)

        def part(dx, p):
            if not 0 <= p < 4:
                return jnp.zeros((64, 128), jnp.float32)
            return product[64 * (dx + 1) : 64 * (dx + 2), 128 * p : 128 * p + 128]

        pieces = []
        for p in range(4):
            below = pltpu.roll(jnp.where(half, part(-1, p), part(-1, p - 1)), 64, 1)
            above = pltpu.roll(jnp.where(half, part(1, p + 1), part(1, p)), 64, 1)
            pieces.append(part(0, p) + below + above)
        conv[i] = jnp.concatenate(pieces, axis=1)
        return carry

    lax.fori_loop(0, count, middle, 0, unroll=2)

    @pl.when(has_left)
    def _():
        rise.wait_recv()
        fall.wait_send()

    @pl.when(has_right)
    def _():
        fall.wait_recv()
        rise.wait_send()

    step = 4

    def edges(g, carry):
        tall = [[], [], [], []]
        for n in range(step):
            i = g * step + n

            def outer(dy, dz):
                return upper[row(i, 1, dy, dz)] * first + lower[row(i, -1, dy, dz)] * second

            edge = (outer(0, 0),) + halos(outer, (low_y[:, :128], low_z[:, :128]))
            for into, piece in zip(tall, edge):
                into.append(piece)
        tall = [jnp.concatenate(m, axis=0) for m in tall]
        stacked = stack(*tall, side_y[...], side_z[...], side_yz[...])
        outside = jnp.concatenate([weight_t[0:64], weight_t[128:192]], axis=0)
        product = dot(outside, stacked)
        for n in range(step):
            i = g * step + n
            mine = product[:, 128 * n : 128 * n + 128]
            turned = pltpu.roll(jnp.where(half, mine[64:], mine[:64]), 64, 1)
            mask = occ_ref[pl.ds(i, 1), :].astype(jnp.float32)
            summed = feat[i].astype(jnp.float32) + conv[i] + shift
            ends = jnp.concatenate(
                [
                    jnp.where(half, turned, 0.0),
                    jnp.zeros((64, 256), jnp.float32),
                    jnp.where(half, 0.0, turned),
                ],
                axis=1,
            )
            fine[i] = (mask * (summed + ends)).astype(jnp.bfloat16)
        return carry

    lax.fori_loop(0, count // step, edges, 0)
    store = pltpu.make_async_copy(fine, fine_hbm, local_sem.at[len(loads)])
    store.start()

    ordered = dot(fine[...].reshape(count * 64, 512), perm[...])
    columns = []
    for j in range(0, count, 2):
        taps = []
        for s in range(4):
            one = ordered[64 * j : 64 * j + 64, 128 * s : 128 * s + 128]
            two = ordered[64 * j + 64 : 64 * j + 128, 128 * s : 128 * s + 128]
            taps.append(jnp.where(half, one, pltpu.roll(two, 64, 1)))
            taps.append(jnp.where(half, pltpu.roll(one, 64, 1), two))
        columns.append(jnp.concatenate(taps, axis=0).astype(jnp.bfloat16))
    octants = dot(flipped(stride[...]), jnp.concatenate(columns, axis=1)) + bias
    octs[...] = octants.astype(jnp.bfloat16)
    swap_octs.start()
    total = place(keys[...], octs[...], device, count)
    swap_keys.wait()
    swap_octs.wait()
    total = total + place(keys_in[...], octs_in[...], device, count)
    coarse_ref[0] = total.astype(jnp.bfloat16)
    store.wait()


def shards(
    features, occupancy, neighbours, coarse_map, norm_gain, time_shift, conv_weight,
    stride_weight, coarse_bias,
):
    count = features.shape[0]
    bf16 = jnp.bfloat16
    vmem = pl.BlockSpec(memory_space=pltpu.VMEM)
    smem = pl.BlockSpec(memory_space=pltpu.SMEM)
    hbm = pl.BlockSpec(memory_space=pl.ANY)
    side_y = window_matrix([(-1, 0), (1, 0)], [0, 1])
    side_z = window_matrix([(0, -1), (0, 1)], [0, 2])
    side_yz = window_matrix([(-1, -1), (-1, 1), (1, -1), (1, 1)], [0, 1, 2, 3])
    return pl.pallas_call(
        kernel,
        out_shape=(
            jax.ShapeDtypeStruct(features.shape, bf16),
            jax.ShapeDtypeStruct((1, 128, 512), bf16),
        ),
        in_specs=[smem] + [vmem] * 5 + [hbm] * 7,
        out_specs=(hbm, vmem),
        scratch_shapes=[
            pltpu.VMEM((count, 64, 512), bf16),
            pltpu.VMEM((1728, 64), bf16),
            pltpu.VMEM((512, 128), bf16),
            pltpu.VMEM((256, 256), bf16),
            pltpu.VMEM((256, 256), bf16),
            pltpu.VMEM((512, 512), bf16),
            pltpu.VMEM((512, 512), bf16),
            pltpu.VMEM((count + 1, 64, 512), bf16),
            pltpu.VMEM((count + 1, 64, 128), bf16),
            pltpu.VMEM((count + 1, 64, 128), bf16),
            pltpu.VMEM((count, 64, 512), jnp.float32),
            pltpu.VMEM((count, 64, 512), bf16),
            pltpu.VMEM((192, 576), bf16),
            pltpu.VMEM((count, 128), jnp.int32),
            pltpu.VMEM((count, 128), jnp.int32),
            pltpu.VMEM((128, 64 * count), bf16),
            pltpu.VMEM((128, 64 * count), bf16),
            pltpu.SemaphoreType.DMA((8,)),
            pltpu.SemaphoreType.DMA((4,)),
            pltpu.SemaphoreType.DMA((4,)),
        ],
        compiler_params=pltpu.CompilerParams(
            collective_id=0, has_side_effects=True, vmem_limit_bytes=48 * 1024 * 1024
        ),
        name="bricks",
    )(
        neighbours, occupancy, coarse_map[None], norm_gain[None], time_shift[None],
        coarse_bias[None], features, conv_weight.reshape(1728, 64),
        stride_weight.reshape(512, 128), side_y, side_z, side_yz, stride_matrix(),
    )


def solution(mesh):
    wide = P(AXES, None, None)
    return jax.shard_map(
        shards,
        mesh=mesh,
        in_specs=(wide, P(AXES, None), P(AXES, None), P(AXES), P(), P(), P(), P(), P()),
        out_specs=(wide, wide),
        check_vma=False,
    )
```

```python
import jax
import jax.numpy as jnp
import numpy as np
from jax import lax
from jax.experimental import pallas as pl
from jax.experimental.pallas import tpu as pltpu
from jax.sharding import PartitionSpec as P

norm_eps = 1e-06
AXES = ("bricks", "grp")


def window_matrix(shifts, kinds):
    table = np.zeros((4, 2, 64, len(shifts), 2, 64), np.float32)
    for w, (b, c) in enumerate(shifts):
        for y in range(8):
            for z in range(8):
                yy, zz = y + b, z + c
                kind = (1 if not 0 <= yy < 8 else 0) + (2 if not 0 <= zz < 8 else 0)
                for half in range(2):
                    table[kind, half, (yy % 8) * 8 + zz % 8, w, half, y * 8 + z] = 1.0
    return table[kinds].reshape(128 * len(kinds), 128 * len(shifts)).astype(jnp.bfloat16)


def stride_matrix():
    table = np.zeros((512, 512), np.float32)
    for x in range(8):
        for y in range(8):
            for z in range(8):
                tap = 4 * (x % 2) + 2 * (y % 2) + z % 2
                place = 16 * (x // 2) + 4 * (y // 2) + z // 2
                table[64 * x + 8 * y + z, 64 * tap + place] = 1.0
    return table.astype(jnp.bfloat16)


def column(row):
    n = row.shape[1]
    at = lax.broadcasted_iota(jnp.int32, (n, n), 0)
    to = lax.broadcasted_iota(jnp.int32, (n, n), 1)
    return jnp.sum(jnp.where(at == to, row, 0.0), axis=1, keepdims=True)


def offset(dx, dy, dz):
    o = 9 * (dx + 1) + 3 * (dy + 1) + dz + 1
    return o - 1 if o > 13 else o


def dot(a, b):
    return jnp.dot(a, b, preferred_element_type=jnp.float32)


def halos(fetch, masks):
    low_y, low_z = masks
    high_y, high_z = 1 - low_y, 1 - low_z
    halo_y = fetch(1, 0) * low_y + fetch(-1, 0) * high_y
    halo_z = fetch(0, 1) * low_z + fetch(0, -1) * high_z
    near = fetch(1, 1) * low_z + fetch(1, -1) * high_z
    far = fetch(-1, 1) * low_z + fetch(-1, -1) * high_z
    return halo_y, halo_z, near * low_y + far * high_y


def flipped(x):
    n = x.shape[1]
    at = lax.broadcasted_iota(jnp.int32, (n, n), 0)
    to = lax.broadcasted_iota(jnp.int32, (n, n), 1)
    eye = jnp.where(at == to, 1.0, 0.0).astype(jnp.bfloat16)
    dims = (((1,), (1,)), ((), ()))
    return lax.dot_general(eye, x, dims, preferred_element_type=jnp.float32).astype(jnp.bfloat16)


def stack(centre, halo_y, halo_z, corner, side_y, side_z, side_yz):
    tiles = centre.shape[0] // 64
    pair_y = dot(jnp.concatenate([centre, halo_y], axis=1), side_y).astype(jnp.bfloat16)
    pair_z = dot(jnp.concatenate([centre, halo_z], axis=1), side_z).astype(jnp.bfloat16)
    four = jnp.concatenate([centre, halo_y, halo_z, corner], axis=1)
    quad = dot(four, side_yz).astype(jnp.bfloat16)
    order = [
        (quad, 0), (pair_y, 0), (quad, 1), (pair_z, 0), (centre, 0),
        (pair_z, 1), (quad, 2), (pair_y, 1), (quad, 3),
    ]
    return jnp.concatenate(
        [
            jnp.concatenate(
                [m[64 * p : 64 * p + 64, 128 * w : 128 * w + 128] for m, w in order], axis=0
            )
            for p in range(tiles)
        ],
        axis=1,
    )


def place(keys, near, far, coarse, count):
    k = lax.broadcasted_iota(jnp.int32, (64, 512), 0)
    lane = lax.broadcasted_iota(jnp.int32, (64, 512), 1)
    rest = lane - (64 * (k >> 4) + 8 * ((k >> 2) & 3) + (k & 3))
    o = keys & 7
    starts = 256 * (o >> 2) + 32 * ((o >> 1) & 1) + 4 * (o & 1)
    starts = jnp.where((keys >> 3) == coarse, starts, -1024)
    starts = jnp.concatenate([starts] * 4, axis=1)
    blocks = [
        jnp.where(rest == starts[j : j + 1], 1.0, 0.0).astype(jnp.bfloat16) for j in range(count)
    ]
    octants = jnp.concatenate([near, far], axis=1)
    return dot(octants, jnp.concatenate(blocks, axis=0))


def kernel(
    occ_hbm, gain_hbm, feat_hbm, map_hbm, near_hbm, weight_hbm, side_y_hbm, side_z_hbm,
    side_yz_hbm, perm_hbm, stride_hbm, shift_hbm, bias_hbm,
    fine_hbm, coarse_hbm,
    occ_ref, gain_ref, feat, map_ref, near_ref, weight, side_y, side_z,
    side_yz, perm, stride, shift_ref, bias_ref,
    act, lower, upper, conv, fine, coarse, weight_t, keys, keys_in, octs, octs_in,
    local_sem, send_sem, recv_sem,
):
    count = feat.shape[0]
    groups = lax.axis_size("grp")
    peers = groups * lax.axis_size("bricks")
    device = lax.axis_index("bricks") * groups + lax.axis_index("grp")
    has_left = device > 0
    has_right = device < peers - 1

    def coords(other):
        return {"bricks": other // groups, "grp": other % groups}

    loads = [
        pltpu.make_async_copy(src, dst, local_sem.at[n])
        for n, (src, dst) in enumerate(
            [
                (occ_hbm, occ_ref), (gain_hbm, gain_ref), (feat_hbm, feat), (map_hbm, map_ref),
                (near_hbm, near_ref), (weight_hbm, weight), (side_y_hbm, side_y),
                (side_z_hbm, side_z), (side_yz_hbm, side_yz), (perm_hbm, perm),
                (stride_hbm, stride), (shift_hbm, shift_ref), (bias_hbm, bias_ref),
            ]
        )
    ]
    for load in loads:
        load.start()
    barrier = pltpu.get_barrier_semaphore()

    @pl.when(has_left)
    def _():
        pl.semaphore_signal(
            barrier, inc=1, device_id=coords(device - 1), device_id_type=pl.DeviceIdType.MESH
        )

    @pl.when(has_right)
    def _():
        pl.semaphore_signal(
            barrier, inc=1, device_id=coords(device + 1), device_id_type=pl.DeviceIdType.MESH
        )

    act[count] = jnp.zeros((64, 512), jnp.bfloat16)
    lower[count] = jnp.zeros((64, 128), jnp.bfloat16)
    upper[count] = jnp.zeros((64, 128), jnp.bfloat16)

    @pl.when(jnp.logical_not(has_left))
    def _():
        lower[0:count] = jnp.zeros((count, 64, 128), jnp.bfloat16)

    @pl.when(jnp.logical_not(has_right))
    def _():
        upper[0:count] = jnp.zeros((count, 64, 128), jnp.bfloat16)

    for load in loads[:3]:
        load.wait()
    gain = column(gain_ref[...])

    def activate_one(i, carry):
        values = feat[i].astype(jnp.float32)
        scale = lax.rsqrt(jnp.mean(values * values, axis=0, keepdims=True) + norm_eps)
        normed = values * scale * gain
        mask = occ_ref[pl.ds(i, 1), :].astype(jnp.float32)
        act[i] = (normed / (1.0 + jnp.exp(-normed)) * mask).astype(jnp.bfloat16)
        return carry

    lax.fori_loop(0, count, activate_one, 0, unroll=2)
    loads[3].wait()
    keys[...] = jnp.broadcast_to(
        column(map_ref[...].astype(jnp.float32)).astype(jnp.int32), keys.shape
    )

    def remote(n, src, dst, other):
        return pltpu.make_async_remote_copy(
            src_ref=src, dst_ref=dst, send_sem=send_sem.at[n], recv_sem=recv_sem.at[n],
            device_id=coords(other), device_id_type=pl.DeviceIdType.MESH,
        )

    bricks = pl.ds(0, count)
    rise = remote(0, act.at[bricks, :, pl.ds(384, 128)], lower.at[bricks], device + 1)
    fall = remote(1, act.at[bricks, :, pl.ds(0, 128)], upper.at[bricks], device - 1)
    mate = device + 1 - 2 * (device % 2)
    swap_keys = remote(2, keys, keys_in, mate)

    pl.semaphore_wait(barrier, has_left.astype(jnp.int32) + has_right.astype(jnp.int32))

    @pl.when(has_right)
    def _():
        rise.start()

    @pl.when(has_left)
    def _():
        fall.start()

    swap_keys.start()

    for load in loads[4:]:
        load.wait()
    shift = column(shift_ref[...])
    bias = column(bias_ref[...])
    stride_t = flipped(stride[...])
    for a in range(3):
        weight_t[64 * a : 64 * a + 64] = flipped(weight[576 * a : 576 * a + 576])

    lane = lax.broadcasted_iota(jnp.int32, (64, 512), 1)
    low_y = jnp.where(lane % 64 < 32, 1.0, 0.0).astype(jnp.bfloat16)
    low_z = jnp.where(lane % 8 < 4, 1.0, 0.0).astype(jnp.bfloat16)
    half = lax.broadcasted_iota(jnp.int32, (64, 128), 1) < 64
    first = jnp.where(half, 1.0, 0.0).astype(jnp.bfloat16)
    second = 1 - first

    def row(i, dx, dy, dz):
        target = near_ref[i, offset(dx, dy, dz)]
        local = jnp.clip(target - (device + dx) * count, 0, count - 1)
        return jnp.where(target < 0, count, local)

    def middle(i, carry):
        def own(dy, dz):
            return act[row(i, 0, dy, dz)]

        wide = (act[i],) + halos(own, (low_y, low_z))
        tall = [
            jnp.concatenate([m[:, 128 * p : 128 * p + 128] for p in range(4)], axis=0)
            for m in wide
        ]
        stacked = stack(*tall, side_y[...], side_z[...], side_yz[...])
        product = dot(weight_t[...], stacked)

        def part(dx, p):
            if not 0 <= p < 4:
                return jnp.zeros((64, 128), jnp.float32)
            return product[64 * (dx + 1) : 64 * (dx + 2), 128 * p : 128 * p + 128]

        pieces = []
        for p in range(4):
            below = pltpu.roll(jnp.where(half, part(-1, p), part(-1, p - 1)), 64, 1)
            above = pltpu.roll(jnp.where(half, part(1, p + 1), part(1, p)), 64, 1)
            pieces.append(part(0, p) + below + above)
        conv[i] = jnp.concatenate(pieces, axis=1)
        return carry

    lax.fori_loop(0, count, middle, 0, unroll=2)

    @pl.when(has_left)
    def _():
        rise.wait_recv()
        fall.wait_send()

    @pl.when(has_right)
    def _():
        fall.wait_recv()
        rise.wait_send()

    step = count // 2
    outside = jnp.concatenate([weight_t[0:64], weight_t[128:192]], axis=0)
    sent = []
    stores = []
    for g in range(2):
        group = pl.ds(g * step, step)
        tall = [[], [], [], []]
        for n in range(step):
            i = g * step + n

            def outer(dy, dz):
                return upper[row(i, 1, dy, dz)] * first + lower[row(i, -1, dy, dz)] * second

            edge = (outer(0, 0),) + halos(outer, (low_y[:, :128], low_z[:, :128]))
            for into, piece in zip(tall, edge):
                into.append(piece)
        tall = [jnp.concatenate(m, axis=0) for m in tall]
        stacked = stack(*tall, side_y[...], side_z[...], side_yz[...])
        product = dot(outside, stacked)
        for n in range(step):
            i = g * step + n
            mine = product[:, 128 * n : 128 * n + 128]
            turned = pltpu.roll(jnp.where(half, mine[64:], mine[:64]), 64, 1)
            mask = occ_ref[pl.ds(i, 1), :].astype(jnp.float32)
            summed = feat[i].astype(jnp.float32) + conv[i] + shift
            ends = jnp.concatenate(
                [
                    jnp.where(half, turned, 0.0),
                    jnp.zeros((64, 256), jnp.float32),
                    jnp.where(half, 0.0, turned),
                ],
                axis=1,
            )
            fine[i] = (mask * (summed + ends)).astype(jnp.bfloat16)
        store = pltpu.make_async_copy(
            fine.at[group], fine_hbm.at[group], local_sem.at[len(loads) + g]
        )
        store.start()
        stores.append(store)

        ordered = dot(fine[group].reshape(step * 64, 512), perm[...])
        columns = []
        for j in range(0, step, 2):
            taps = []
            for s in range(4):
                one = ordered[64 * j : 64 * j + 64, 128 * s : 128 * s + 128]
                two = ordered[64 * j + 64 : 64 * j + 128, 128 * s : 128 * s + 128]
                taps.append(jnp.where(half, one, pltpu.roll(two, 64, 1)))
                taps.append(jnp.where(half, pltpu.roll(one, 64, 1), two))
            columns.append(jnp.concatenate(taps, axis=0).astype(jnp.bfloat16))
        octants = dot(stride_t, jnp.concatenate(columns, axis=1)) + bias
        octs[g] = octants.astype(jnp.bfloat16)
        swap = remote(3 + g, octs.at[g], octs_in.at[g], mate)
        swap.start()
        sent.append(swap)

    total = place(keys[...], octs[0], octs[1], device, count)
    swap_keys.wait()
    for swap in sent:
        swap.wait()
    total = total + place(keys_in[...], octs_in[0], octs_in[1], device, count)
    coarse[0] = total.astype(jnp.bfloat16)
    store = pltpu.make_async_copy(coarse, coarse_hbm, local_sem.at[len(loads) + 2])
    store.start()
    for store in stores + [store]:
        store.wait()


def shards(
    features, occupancy, neighbours, coarse_map, norm_gain, time_shift, conv_weight,
    stride_weight, coarse_bias,
):
    count = features.shape[0]
    bf16 = jnp.bfloat16
    hbm = pl.BlockSpec(memory_space=pl.ANY)
    side_y = window_matrix([(-1, 0), (1, 0)], [0, 1])
    side_z = window_matrix([(0, -1), (0, 1)], [0, 2])
    side_yz = window_matrix([(-1, -1), (-1, 1), (1, -1), (1, 1)], [0, 1, 2, 3])
    return pl.pallas_call(
        kernel,
        out_shape=(
            jax.ShapeDtypeStruct(features.shape, bf16),
            jax.ShapeDtypeStruct((1, 128, 512), bf16),
        ),
        in_specs=[hbm] * 13,
        out_specs=(hbm, hbm),
        scratch_shapes=[
            pltpu.VMEM((count, 512), jnp.int32),
            pltpu.VMEM((1, 64), jnp.float32),
            pltpu.VMEM((count, 64, 512), bf16),
            pltpu.VMEM((1, count), jnp.int32),
            pltpu.SMEM((count, 26), jnp.int32),
            pltpu.VMEM((1728, 64), bf16),
            pltpu.VMEM((256, 256), bf16),
            pltpu.VMEM((256, 256), bf16),
            pltpu.VMEM((512, 512), bf16),
            pltpu.VMEM((512, 512), bf16),
            pltpu.VMEM((512, 128), bf16),
            pltpu.VMEM((1, 64), jnp.float32),
            pltpu.VMEM((1, 128), jnp.float32),
            pltpu.VMEM((count + 1, 64, 512), bf16),
            pltpu.VMEM((count + 1, 64, 128), bf16),
            pltpu.VMEM((count + 1, 64, 128), bf16),
            pltpu.VMEM((count, 64, 512), jnp.float32),
            pltpu.VMEM((count, 64, 512), bf16),
            pltpu.VMEM((1, 128, 512), bf16),
            pltpu.VMEM((192, 576), bf16),
            pltpu.VMEM((count, 128), jnp.int32),
            pltpu.VMEM((count, 128), jnp.int32),
            pltpu.VMEM((2, 128, 32 * count), bf16),
            pltpu.VMEM((2, 128, 32 * count), bf16),
            pltpu.SemaphoreType.DMA((16,)),
            pltpu.SemaphoreType.DMA((5,)),
            pltpu.SemaphoreType.DMA((5,)),
        ],
        compiler_params=pltpu.CompilerParams(
            collective_id=0, has_side_effects=True, vmem_limit_bytes=63 * 1024 * 1024
        ),
        name="bricks",
    )(
        occupancy, norm_gain[None], features, coarse_map[None], neighbours,
        conv_weight.reshape(1728, 64), side_y, side_z, side_yz, stride_matrix(),
        stride_weight.reshape(512, 128), time_shift[None], coarse_bias[None],
    )


def solution(mesh):
    wide = P(AXES, None, None)
    return jax.shard_map(
        shards,
        mesh=mesh,
        in_specs=(wide, P(AXES, None), P(AXES, None), P(AXES), P(), P(), P(), P(), P()),
        out_specs=(wide, wide),
        check_vma=False,
    )
```

```python
import jax
import jax.numpy as jnp
import numpy as np
from jax import lax
from jax.experimental import pallas as pl
from jax.experimental.pallas import tpu as pltpu
from jax.sharding import PartitionSpec as P

norm_eps = 1e-06
AXES = ("bricks", "grp")


def shift_matrix(dim):
    table = np.zeros((2, 2, 8, 8, 2, 2, 8, 8), np.float32)
    for w, shift in enumerate((-1, 1)):
        for y in range(8):
            for z in range(8):
                at = [y, z]
                at[dim] += shift
                kind = 0 if 0 <= at[dim] < 8 else 1
                for half in range(2):
                    table[kind, half, at[0] % 8, at[1] % 8, w, half, y, z] = 1.0
    return table.reshape(256, 256).astype(jnp.bfloat16)


def stride_matrix():
    table = np.zeros((512, 512), np.float32)
    for x in range(8):
        for y in range(8):
            for z in range(8):
                tap = 4 * (x % 2) + 2 * (y % 2) + z % 2
                place = 16 * (x // 2) + 4 * (y // 2) + z // 2
                table[64 * x + 8 * y + z, 64 * tap + place] = 1.0
    return table.astype(jnp.bfloat16)


def column(row):
    n = row.shape[1]
    at = lax.broadcasted_iota(jnp.int32, (n, n), 0)
    to = lax.broadcasted_iota(jnp.int32, (n, n), 1)
    return jnp.sum(jnp.where(at == to, row, 0.0), axis=1, keepdims=True)


def offset(dx, dy, dz):
    o = 9 * (dx + 1) + 3 * (dy + 1) + dz + 1
    return o - 1 if o > 13 else o


def dot(a, b):
    return jnp.dot(a, b, preferred_element_type=jnp.float32)


def halos(fetch, masks):
    low_y, low_z = masks
    high_y, high_z = 1 - low_y, 1 - low_z
    halo_y = fetch(1, 0) * low_y + fetch(-1, 0) * high_y
    halo_z = fetch(0, 1) * low_z + fetch(0, -1) * high_z
    near = fetch(1, 1) * low_z + fetch(1, -1) * high_z
    far = fetch(-1, 1) * low_z + fetch(-1, -1) * high_z
    return halo_y, halo_z, near * low_y + far * high_y


def flipped(x):
    n = x.shape[1]
    at = lax.broadcasted_iota(jnp.int32, (n, n), 0)
    to = lax.broadcasted_iota(jnp.int32, (n, n), 1)
    eye = jnp.where(at == to, 1.0, 0.0).astype(jnp.bfloat16)
    dims = (((1,), (1,)), ((), ()))
    return lax.dot_general(eye, x, dims, preferred_element_type=jnp.float32).astype(jnp.bfloat16)


def stack(centre, halo_y, halo_z, corner, side_y, side_z):
    rows = centre.shape[0]
    tiles = rows // 64
    own = jnp.concatenate([centre, halo_y], axis=1)
    rim = jnp.concatenate([halo_z, corner], axis=1)
    moved = dot(jnp.concatenate([own, rim], axis=0), side_y).astype(jnp.bfloat16)
    planes = [moved[:rows, :128], centre, moved[:rows, 128:]]
    rims = [moved[rows:, :128], halo_z, moved[rows:, 128:]]
    pairs = [jnp.concatenate([a, b], axis=1) for a, b in zip(planes, rims)]
    turned = dot(jnp.concatenate(pairs, axis=0), side_z).astype(jnp.bfloat16)
    order = []
    for b in range(3):
        part = turned[rows * b : rows * (b + 1)]
        order += [part[:, :128], planes[b], part[:, 128:]]
    return jnp.concatenate(
        [
            jnp.concatenate([m[64 * p : 64 * p + 64] for m in order], axis=0)
            for p in range(tiles)
        ],
        axis=1,
    )


def place(keys, near, far, coarse, count):
    k = lax.broadcasted_iota(jnp.int32, (64, 512), 0)
    lane = lax.broadcasted_iota(jnp.int32, (64, 512), 1)
    rest = lane - (64 * (k >> 4) + 8 * ((k >> 2) & 3) + (k & 3))
    o = keys & 7
    starts = 256 * (o >> 2) + 32 * ((o >> 1) & 1) + 4 * (o & 1)
    starts = jnp.where((keys >> 3) == coarse, starts, -1024)
    starts = jnp.concatenate([starts] * 4, axis=1)
    blocks = [
        jnp.where(rest == starts[j : j + 1], 1.0, 0.0).astype(jnp.bfloat16) for j in range(count)
    ]
    octants = jnp.concatenate([near, far], axis=1)
    return dot(octants, jnp.concatenate(blocks, axis=0))


def kernel(
    occ_hbm, gain_hbm, feat_hbm, map_hbm, near_hbm, weight_hbm, side_y_hbm, side_z_hbm,
    perm_hbm, stride_hbm, shift_hbm, bias_hbm,
    fine, keys, keys_in, octs, octs_in,
    occ_ref, gain_ref, feat, map_ref, near_ref, weight, side_y, side_z,
    perm, stride, shift_ref, bias_ref,
    act, lower, upper, conv, weight_t,
    local_sem, send_sem, recv_sem,
):
    count = feat.shape[0]
    groups = lax.axis_size("grp")
    peers = groups * lax.axis_size("bricks")
    device = lax.axis_index("bricks") * groups + lax.axis_index("grp")
    has_left = device > 0
    has_right = device < peers - 1

    def coords(other):
        return {"bricks": other // groups, "grp": other % groups}

    loads = [
        pltpu.make_async_copy(src, dst, local_sem.at[n])
        for n, (src, dst) in enumerate(
            [
                (occ_hbm, occ_ref), (gain_hbm, gain_ref), (feat_hbm, feat), (map_hbm, map_ref),
                (near_hbm, near_ref), (weight_hbm, weight), (side_y_hbm, side_y),
                (side_z_hbm, side_z), (perm_hbm, perm),
                (stride_hbm, stride), (shift_hbm, shift_ref), (bias_hbm, bias_ref),
            ]
        )
    ]
    for load in loads:
        load.start()
    barrier = pltpu.get_barrier_semaphore()

    @pl.when(has_left)
    def _():
        pl.semaphore_signal(
            barrier, inc=1, device_id=coords(device - 1), device_id_type=pl.DeviceIdType.MESH
        )

    @pl.when(has_right)
    def _():
        pl.semaphore_signal(
            barrier, inc=1, device_id=coords(device + 1), device_id_type=pl.DeviceIdType.MESH
        )

    act[count] = jnp.zeros((64, 512), jnp.bfloat16)
    lower[count] = jnp.zeros((64, 128), jnp.bfloat16)
    upper[count] = jnp.zeros((64, 128), jnp.bfloat16)

    @pl.when(jnp.logical_not(has_left))
    def _():
        lower[0:count] = jnp.zeros((count, 64, 128), jnp.bfloat16)

    @pl.when(jnp.logical_not(has_right))
    def _():
        upper[0:count] = jnp.zeros((count, 64, 128), jnp.bfloat16)

    for load in loads[:3]:
        load.wait()
    gain = column(gain_ref[...])

    def activate_one(i, carry):
        values = feat[i].astype(jnp.float32)
        scale = lax.rsqrt(jnp.mean(values * values, axis=0, keepdims=True) + norm_eps)
        normed = values * scale * gain
        mask = occ_ref[pl.ds(i, 1), :].astype(jnp.float32)
        act[i] = (normed * (mask * 0.5) * (1.0 + jnp.tanh(0.5 * normed))).astype(jnp.bfloat16)
        return carry

    lax.fori_loop(0, count, activate_one, 0, unroll=2)
    loads[3].wait()
    keys[...] = jnp.broadcast_to(
        column(map_ref[...].astype(jnp.float32)).astype(jnp.int32), keys.shape
    )

    def remote(n, src, dst, other):
        return pltpu.make_async_remote_copy(
            src_ref=src, dst_ref=dst, send_sem=send_sem.at[n], recv_sem=recv_sem.at[n],
            device_id=coords(other), device_id_type=pl.DeviceIdType.MESH,
        )

    bricks = pl.ds(0, count)
    rise = remote(0, act.at[bricks, :, pl.ds(384, 128)], lower.at[bricks], device + 1)
    fall = remote(1, act.at[bricks, :, pl.ds(0, 128)], upper.at[bricks], device - 1)
    mate = device + 1 - 2 * (device % 2)
    swap_keys = remote(2, keys, keys_in, mate)

    pl.semaphore_wait(barrier, has_left.astype(jnp.int32) + has_right.astype(jnp.int32))

    @pl.when(has_right)
    def _():
        rise.start()

    @pl.when(has_left)
    def _():
        fall.start()

    swap_keys.start()

    for load in loads[4:]:
        load.wait()
    shift = column(shift_ref[...])
    bias = column(bias_ref[...])
    stride_t = flipped(stride[...])
    for a in range(3):
        weight_t[64 * a : 64 * a + 64] = flipped(weight[576 * a : 576 * a + 576])

    lane = lax.broadcasted_iota(jnp.int32, (64, 512), 1)
    low_y = jnp.where(lane % 64 < 32, 1.0, 0.0).astype(jnp.bfloat16)
    low_z = jnp.where(lane % 8 < 4, 1.0, 0.0).astype(jnp.bfloat16)
    half = lax.broadcasted_iota(jnp.int32, (64, 128), 1) < 64
    first = jnp.where(half, 1.0, 0.0).astype(jnp.bfloat16)
    second = 1 - first

    def row(i, dx, dy, dz):
        target = near_ref[i, offset(dx, dy, dz)]
        local = jnp.clip(target - (device + dx) * count, 0, count - 1)
        return jnp.where(target < 0, count, local)

    def middle(i, carry):
        def own(dy, dz):
            return act[row(i, 0, dy, dz)]

        wide = (act[i],) + halos(own, (low_y, low_z))
        tall = [
            jnp.concatenate([m[:, 128 * p : 128 * p + 128] for p in range(4)], axis=0)
            for m in wide
        ]
        stacked = stack(*tall, side_y[...], side_z[...])
        product = dot(weight_t[...], stacked)

        def part(dx, p):
            if not 0 <= p < 4:
                return jnp.zeros((64, 128), jnp.float32)
            return product[64 * (dx + 1) : 64 * (dx + 2), 128 * p : 128 * p + 128]

        pieces = []
        for p in range(4):
            below = pltpu.roll(jnp.where(half, part(-1, p), part(-1, p - 1)), 64, 1)
            above = pltpu.roll(jnp.where(half, part(1, p + 1), part(1, p)), 64, 1)
            pieces.append(part(0, p) + below + above)
        conv[i] = jnp.concatenate(pieces, axis=1)
        return carry

    lax.fori_loop(0, count, middle, 0, unroll=2)

    @pl.when(has_left)
    def _():
        rise.wait_recv()
        fall.wait_send()

    @pl.when(has_right)
    def _():
        fall.wait_recv()
        rise.wait_send()

    step = count // 2
    outside = jnp.concatenate([weight_t[0:64], weight_t[128:192]], axis=0)
    sent = []
    for g in range(2):
        group = pl.ds(g * step, step)
        tall = [[], [], [], []]
        for n in range(step):
            i = g * step + n

            def outer(dy, dz):
                return upper[row(i, 1, dy, dz)] * first + lower[row(i, -1, dy, dz)] * second

            edge = (outer(0, 0),) + halos(outer, (low_y[:, :128], low_z[:, :128]))
            for into, piece in zip(tall, edge):
                into.append(piece)
        tall = [jnp.concatenate(m, axis=0) for m in tall]
        stacked = stack(*tall, side_y[...], side_z[...])
        product = dot(outside, stacked)
        for n in range(step):
            i = g * step + n
            mine = product[:, 128 * n : 128 * n + 128]
            turned = pltpu.roll(jnp.where(half, mine[64:], mine[:64]), 64, 1)
            mask = occ_ref[pl.ds(i, 1), :].astype(jnp.float32)
            summed = feat[i].astype(jnp.float32) + conv[i] + shift
            ends = jnp.concatenate(
                [
                    jnp.where(half, turned, 0.0),
                    jnp.zeros((64, 256), jnp.float32),
                    jnp.where(half, 0.0, turned),
                ],
                axis=1,
            )
            fine[i] = (mask * (summed + ends)).astype(jnp.bfloat16)
        ordered = dot(fine[group].reshape(step * 64, 512), perm[...])
        columns = []
        for j in range(0, step, 2):
            taps = []
            for s in range(4):
                one = ordered[64 * j : 64 * j + 64, 128 * s : 128 * s + 128]
                two = ordered[64 * j + 64 : 64 * j + 128, 128 * s : 128 * s + 128]
                taps.append(jnp.where(half, one, pltpu.roll(two, 64, 1)))
                taps.append(jnp.where(half, pltpu.roll(one, 64, 1), two))
            columns.append(jnp.concatenate(taps, axis=0).astype(jnp.bfloat16))
        octants = dot(stride_t, jnp.concatenate(columns, axis=1)) + bias
        octs[g] = octants.astype(jnp.bfloat16)
        swap = remote(3 + g, octs.at[g], octs_in.at[g], mate)
        swap.start()
        sent.append(swap)

    swap_keys.wait()
    for swap in sent:
        swap.wait()


def finish(fine, keys, keys_in, octs, octs_in, fine_hbm, coarse_hbm, coarse, sem):
    count = fine.shape[0]
    device = lax.axis_index("bricks") * lax.axis_size("grp") + lax.axis_index("grp")
    store = pltpu.make_async_copy(fine, fine_hbm, sem.at[0])
    store.start()
    total = place(keys[...], octs[0], octs[1], device, count)
    total = total + place(keys_in[...], octs_in[0], octs_in[1], device, count)
    coarse[0] = total.astype(jnp.bfloat16)
    last = pltpu.make_async_copy(coarse, coarse_hbm, sem.at[1])
    last.start()
    store.wait()
    last.wait()


def shards(
    features, occupancy, neighbours, coarse_map, norm_gain, time_shift, conv_weight,
    stride_weight, coarse_bias,
):
    count = features.shape[0]
    bf16 = jnp.bfloat16
    hbm = pl.BlockSpec(memory_space=pltpu.HBM)
    vmem = pl.BlockSpec(memory_space=pltpu.VMEM)
    side_y, side_z = shift_matrix(0), shift_matrix(1)
    found = pl.pallas_call(
        kernel,
        out_shape=(
            jax.ShapeDtypeStruct(features.shape, bf16),
            jax.ShapeDtypeStruct((count, 128), jnp.int32),
            jax.ShapeDtypeStruct((count, 128), jnp.int32),
            jax.ShapeDtypeStruct((2, 128, 32 * count), bf16),
            jax.ShapeDtypeStruct((2, 128, 32 * count), bf16),
        ),
        in_specs=[hbm] * 12,
        out_specs=(vmem,) * 5,
        scratch_shapes=[
            pltpu.VMEM((count, 512), jnp.int32),
            pltpu.VMEM((1, 64), jnp.float32),
            pltpu.VMEM((count, 64, 512), bf16),
            pltpu.VMEM((1, count), jnp.int32),
            pltpu.SMEM((count, 26), jnp.int32),
            pltpu.VMEM((1728, 64), bf16),
            pltpu.VMEM((256, 256), bf16),
            pltpu.VMEM((256, 256), bf16),
            pltpu.VMEM((512, 512), bf16),
            pltpu.VMEM((512, 128), bf16),
            pltpu.VMEM((1, 64), jnp.float32),
            pltpu.VMEM((1, 128), jnp.float32),
            pltpu.VMEM((count + 1, 64, 512), bf16),
            pltpu.VMEM((count + 1, 64, 128), bf16),
            pltpu.VMEM((count + 1, 64, 128), bf16),
            pltpu.VMEM((count, 64, 512), jnp.float32),
            pltpu.VMEM((192, 576), bf16),
            pltpu.SemaphoreType.DMA((16,)),
            pltpu.SemaphoreType.DMA((5,)),
            pltpu.SemaphoreType.DMA((5,)),
        ],
        compiler_params=pltpu.CompilerParams(
            collective_id=0, has_side_effects=True, vmem_limit_bytes=32 * 1024 * 1024
        ),
        name="bricks",
    )(*[
        pltpu.with_memory_space_constraint(x, pltpu.HBM)
        for x in (
            occupancy, norm_gain[None], features, coarse_map[None], neighbours,
            conv_weight.reshape(1728, 64), side_y, side_z, stride_matrix(),
            stride_weight.reshape(512, 128), time_shift[None], coarse_bias[None],
        )
    ])
    return pl.pallas_call(
        finish,
        out_shape=(
            jax.ShapeDtypeStruct(features.shape, bf16),
            jax.ShapeDtypeStruct((1, 128, 512), bf16),
        ),
        in_specs=[vmem] * 5,
        out_specs=(hbm, hbm),
        scratch_shapes=[pltpu.VMEM((1, 128, 512), bf16), pltpu.SemaphoreType.DMA((2,))],
        compiler_params=pltpu.CompilerParams(vmem_limit_bytes=16 * 1024 * 1024),
        name="finish",
    )(*found)


def solution(mesh):
    wide = P(AXES, None, None)
    return jax.shard_map(
        shards,
        mesh=mesh,
        in_specs=(wide, P(AXES, None), P(AXES, None), P(AXES), P(), P(), P(), P(), P()),
        out_specs=(wide, wide),
        check_vma=False,
    )
```

```python
import jax
import jax.numpy as jnp
import numpy as np
from jax import lax
from jax.experimental import pallas as pl
from jax.experimental.pallas import tpu as pltpu
from jax.sharding import PartitionSpec as P

norm_eps = 1e-06
AXES = ("bricks", "grp")


def stride_matrix():
    table = np.zeros((512, 512), np.float32)
    for x in range(8):
        for y in range(8):
            for z in range(8):
                tap = 4 * (x % 2) + 2 * (y % 2) + z % 2
                place = 16 * (x // 2) + 4 * (y // 2) + z // 2
                table[64 * x + 8 * y + z, 64 * tap + place] = 1.0
    return table.astype(jnp.bfloat16)


def column(row):
    n = row.shape[1]
    at = lax.broadcasted_iota(jnp.int32, (n, n), 0)
    to = lax.broadcasted_iota(jnp.int32, (n, n), 1)
    return jnp.sum(jnp.where(at == to, row, 0.0), axis=1, keepdims=True)


def offset(dx, dy, dz):
    o = 9 * (dx + 1) + 3 * (dy + 1) + dz + 1
    return o - 1 if o > 13 else o


def dot(a, b):
    return jnp.dot(a, b, preferred_element_type=jnp.float32)


def halos(fetch, y_low, z_low):
    halo_y = jnp.where(y_low, fetch(1, 0), fetch(-1, 0))
    halo_z = jnp.where(z_low, fetch(0, 1), fetch(0, -1))
    near = jnp.where(z_low, fetch(1, 1), fetch(1, -1))
    far = jnp.where(z_low, fetch(-1, 1), fetch(-1, -1))
    return halo_y, halo_z, jnp.where(y_low, near, far)


def turn(x, by):
    return pltpu.roll(x, by % 128, 1)


def flipped(x):
    n = x.shape[1]
    at = lax.broadcasted_iota(jnp.int32, (n, n), 0)
    to = lax.broadcasted_iota(jnp.int32, (n, n), 1)
    eye = jnp.where(at == to, 1.0, 0.0).astype(jnp.bfloat16)
    dims = (((1,), (1,)), ((), ()))
    return lax.dot_general(eye, x, dims, preferred_element_type=jnp.float32).astype(jnp.bfloat16)


def stack(own, halo_y, halo_z, corner, ends):
    y_first, y_last, z_first, z_last = ends

    def along_y(x, halo):
        far = turn(halo, 64)
        return (
            turn(jnp.where(y_last, far, x), 8), x, turn(jnp.where(y_first, far, x), -8),
        )

    order = []
    for plane, rim in zip(along_y(own, halo_y), along_y(halo_z, corner)):
        order.append(turn(jnp.where(z_last, turn(rim, -8), plane), 1))
        order.append(plane)
        order.append(turn(jnp.where(z_first, turn(rim, 8), plane), -1))
    return jnp.concatenate(order, axis=0)


def place(keys, near, far, coarse, count):
    k = lax.broadcasted_iota(jnp.int32, (64, 512), 0)
    lane = lax.broadcasted_iota(jnp.int32, (64, 512), 1)
    rest = lane - (64 * (k >> 4) + 8 * ((k >> 2) & 3) + (k & 3))
    o = keys & 7
    starts = 256 * (o >> 2) + 32 * ((o >> 1) & 1) + 4 * (o & 1)
    starts = jnp.where((keys >> 3) == coarse, starts, -1024)
    starts = jnp.concatenate([starts] * 4, axis=1)
    blocks = [
        jnp.where(rest == starts[j : j + 1], 1.0, 0.0).astype(jnp.bfloat16) for j in range(count)
    ]
    octants = jnp.concatenate([near, far], axis=1)
    return dot(octants, jnp.concatenate(blocks, axis=0))


def kernel(
    occ_hbm, gain_hbm, feat_hbm, map_hbm, near_hbm, weight_hbm, perm_hbm,
    stride_hbm, shift_hbm, bias_hbm,
    fine, keys, keys_in, octs, octs_in,
    occ_ref, gain_ref, feat, map_ref, near_ref, weight, perm,
    stride, shift_ref, bias_ref,
    act, lower, upper, conv, weight_t,
    local_sem, send_sem, recv_sem,
):
    count = feat.shape[0]
    groups = lax.axis_size("grp")
    peers = groups * lax.axis_size("bricks")
    device = lax.axis_index("bricks") * groups + lax.axis_index("grp")
    has_left = device > 0
    has_right = device < peers - 1

    def coords(other):
        return {"bricks": other // groups, "grp": other % groups}

    loads = [
        pltpu.make_async_copy(src, dst, local_sem.at[n])
        for n, (src, dst) in enumerate(
            [
                (occ_hbm, occ_ref), (gain_hbm, gain_ref), (feat_hbm, feat), (map_hbm, map_ref),
                (near_hbm, near_ref), (weight_hbm, weight), (perm_hbm, perm),
                (stride_hbm, stride), (shift_hbm, shift_ref), (bias_hbm, bias_ref),
            ]
        )
    ]
    for load in loads:
        load.start()
    barrier = pltpu.get_barrier_semaphore()

    @pl.when(has_left)
    def _():
        pl.semaphore_signal(
            barrier, inc=1, device_id=coords(device - 1), device_id_type=pl.DeviceIdType.MESH
        )

    @pl.when(has_right)
    def _():
        pl.semaphore_signal(
            barrier, inc=1, device_id=coords(device + 1), device_id_type=pl.DeviceIdType.MESH
        )

    act[count] = jnp.zeros((64, 512), jnp.bfloat16)
    lower[count] = jnp.zeros((64, 128), jnp.bfloat16)
    upper[count] = jnp.zeros((64, 128), jnp.bfloat16)

    @pl.when(jnp.logical_not(has_left))
    def _():
        lower[0:count] = jnp.zeros((count, 64, 128), jnp.bfloat16)

    @pl.when(jnp.logical_not(has_right))
    def _():
        upper[0:count] = jnp.zeros((count, 64, 128), jnp.bfloat16)

    for load in loads[:3]:
        load.wait()
    gain = column(gain_ref[...])

    def activate_one(i, carry):
        values = feat[i].astype(jnp.float32)
        scale = lax.rsqrt(jnp.mean(values * values, axis=0, keepdims=True) + norm_eps)
        normed = values * scale * gain
        mask = occ_ref[pl.ds(i, 1), :].astype(jnp.float32)
        act[i] = (normed * (mask * 0.5) * (1.0 + jnp.tanh(0.5 * normed))).astype(jnp.bfloat16)
        return carry

    lax.fori_loop(0, count, activate_one, 0, unroll=2)
    loads[3].wait()
    keys[...] = jnp.broadcast_to(
        column(map_ref[...].astype(jnp.float32)).astype(jnp.int32), keys.shape
    )

    def remote(n, src, dst, other):
        return pltpu.make_async_remote_copy(
            src_ref=src, dst_ref=dst, send_sem=send_sem.at[n], recv_sem=recv_sem.at[n],
            device_id=coords(other), device_id_type=pl.DeviceIdType.MESH,
        )

    bricks = pl.ds(0, count)
    rise = remote(0, act.at[bricks, :, pl.ds(384, 128)], lower.at[bricks], device + 1)
    fall = remote(1, act.at[bricks, :, pl.ds(0, 128)], upper.at[bricks], device - 1)
    mate = device + 1 - 2 * (device % 2)
    swap_keys = remote(2, keys, keys_in, mate)

    pl.semaphore_wait(barrier, has_left.astype(jnp.int32) + has_right.astype(jnp.int32))

    @pl.when(has_right)
    def _():
        rise.start()

    @pl.when(has_left)
    def _():
        fall.start()

    swap_keys.start()

    for load in loads[4:]:
        load.wait()
    shift = column(shift_ref[...])
    bias = column(bias_ref[...])
    stride_t = flipped(stride[...])
    for a in range(3):
        weight_t[64 * a : 64 * a + 64] = flipped(weight[576 * a : 576 * a + 576])

    lane = lax.broadcasted_iota(jnp.int32, (64, 128), 1)
    half = lane < 64
    y_low = (lane & 63) < 32
    z_low = (lane & 7) < 4
    marks = ((lane & 63) < 8, (lane & 63) >= 56, (lane & 7) == 0, (lane & 7) == 7)

    def row(i, dx, dy, dz):
        target = near_ref[i, offset(dx, dy, dz)]
        local = jnp.clip(target - (device + dx) * count, 0, count - 1)
        return jnp.where(target < 0, count, local)

    def middle(i, carry):
        rows = {
            (dy, dz): row(i, 0, dy, dz)
            for dy in (-1, 0, 1) for dz in (-1, 0, 1) if (dy, dz) != (0, 0)
        }
        columns = []
        for p in range(4):

            def own(dy, dz):
                return act[rows[dy, dz], :, 128 * p : 128 * p + 128]

            tile = act[i, :, 128 * p : 128 * p + 128]
            columns.append(stack(tile, *halos(own, y_low, z_low), marks))
        product = dot(weight_t[...], jnp.concatenate(columns, axis=1))

        def part(dx, p):
            if not 0 <= p < 4:
                return jnp.zeros((64, 128), jnp.float32)
            return product[64 * (dx + 1) : 64 * (dx + 2), 128 * p : 128 * p + 128]

        pieces = []
        for p in range(4):
            below = pltpu.roll(jnp.where(half, part(-1, p), part(-1, p - 1)), 64, 1)
            above = pltpu.roll(jnp.where(half, part(1, p + 1), part(1, p)), 64, 1)
            pieces.append(part(0, p) + below + above)
        conv[i] = jnp.concatenate(pieces, axis=1)
        return carry

    lax.fori_loop(0, count, middle, 0, unroll=2)

    @pl.when(has_left)
    def _():
        rise.wait_recv()
        fall.wait_send()

    @pl.when(has_right)
    def _():
        fall.wait_recv()
        rise.wait_send()

    step = count // 2
    outside = jnp.concatenate([weight_t[0:64], weight_t[128:192]], axis=0)
    sent = []
    for g in range(2):
        group = pl.ds(g * step, step)
        tall = []
        for n in range(step):
            i = g * step + n

            def outer(dy, dz):
                return jnp.where(half, upper[row(i, 1, dy, dz)], lower[row(i, -1, dy, dz)])

            tall.append(stack(outer(0, 0), *halos(outer, y_low, z_low), marks))
        stacked = jnp.concatenate(tall, axis=1)
        product = dot(outside, stacked)
        for n in range(step):
            i = g * step + n
            mine = product[:, 128 * n : 128 * n + 128]
            turned = pltpu.roll(jnp.where(half, mine[64:], mine[:64]), 64, 1)
            mask = occ_ref[pl.ds(i, 1), :].astype(jnp.float32)
            summed = feat[i].astype(jnp.float32) + conv[i] + shift
            ends = jnp.concatenate(
                [
                    jnp.where(half, turned, 0.0),
                    jnp.zeros((64, 256), jnp.float32),
                    jnp.where(half, 0.0, turned),
                ],
                axis=1,
            )
            fine[i] = (mask * (summed + ends)).astype(jnp.bfloat16)
        ordered = dot(fine[group].reshape(step * 64, 512), perm[...])
        columns = []
        for j in range(0, step, 2):
            taps = []
            for s in range(4):
                one = ordered[64 * j : 64 * j + 64, 128 * s : 128 * s + 128]
                two = ordered[64 * j + 64 : 64 * j + 128, 128 * s : 128 * s + 128]
                taps.append(jnp.where(half, one, pltpu.roll(two, 64, 1)))
                taps.append(jnp.where(half, pltpu.roll(one, 64, 1), two))
            columns.append(jnp.concatenate(taps, axis=0).astype(jnp.bfloat16))
        octants = dot(stride_t, jnp.concatenate(columns, axis=1)) + bias
        octs[g] = octants.astype(jnp.bfloat16)
        swap = remote(3 + g, octs.at[g], octs_in.at[g], mate)
        swap.start()
        sent.append(swap)

    swap_keys.wait()
    for swap in sent:
        swap.wait()


def finish(fine, keys, keys_in, octs, octs_in, fine_hbm, coarse_hbm, coarse, sem):
    count = fine.shape[0]
    device = lax.axis_index("bricks") * lax.axis_size("grp") + lax.axis_index("grp")
    store = pltpu.make_async_copy(fine, fine_hbm, sem.at[0])
    store.start()
    total = place(keys[...], octs[0], octs[1], device, count)
    total = total + place(keys_in[...], octs_in[0], octs_in[1], device, count)
    coarse[0] = total.astype(jnp.bfloat16)
    last = pltpu.make_async_copy(coarse, coarse_hbm, sem.at[1])
    last.start()
    store.wait()
    last.wait()


def shards(
    features, occupancy, neighbours, coarse_map, norm_gain, time_shift, conv_weight,
    stride_weight, coarse_bias,
):
    count = features.shape[0]
    bf16 = jnp.bfloat16
    hbm = pl.BlockSpec(memory_space=pltpu.HBM)
    vmem = pl.BlockSpec(memory_space=pltpu.VMEM)
    found = pl.pallas_call(
        kernel,
        out_shape=(
            jax.ShapeDtypeStruct(features.shape, bf16),
            jax.ShapeDtypeStruct((count, 128), jnp.int32),
            jax.ShapeDtypeStruct((count, 128), jnp.int32),
            jax.ShapeDtypeStruct((2, 128, 32 * count), bf16),
            jax.ShapeDtypeStruct((2, 128, 32 * count), bf16),
        ),
        in_specs=[hbm] * 10,
        out_specs=(vmem,) * 5,
        scratch_shapes=[
            pltpu.VMEM((count, 512), jnp.int32),
            pltpu.VMEM((1, 64), jnp.float32),
            pltpu.VMEM((count, 64, 512), bf16),
            pltpu.VMEM((1, count), jnp.int32),
            pltpu.SMEM((count, 26), jnp.int32),
            pltpu.VMEM((1728, 64), bf16),
            pltpu.VMEM((512, 512), bf16),
            pltpu.VMEM((512, 128), bf16),
            pltpu.VMEM((1, 64), jnp.float32),
            pltpu.VMEM((1, 128), jnp.float32),
            pltpu.VMEM((count + 1, 64, 512), bf16),
            pltpu.VMEM((count + 1, 64, 128), bf16),
            pltpu.VMEM((count + 1, 64, 128), bf16),
            pltpu.VMEM((count, 64, 512), jnp.float32),
            pltpu.VMEM((192, 576), bf16),
            pltpu.SemaphoreType.DMA((16,)),
            pltpu.SemaphoreType.DMA((5,)),
            pltpu.SemaphoreType.DMA((5,)),
        ],
        compiler_params=pltpu.CompilerParams(
            collective_id=0, has_side_effects=True, vmem_limit_bytes=32 * 1024 * 1024
        ),
        name="bricks",
    )(*[
        pltpu.with_memory_space_constraint(x, pltpu.HBM)
        for x in (
            occupancy, norm_gain[None], features, coarse_map[None], neighbours,
            conv_weight.reshape(1728, 64), stride_matrix(),
            stride_weight.reshape(512, 128), time_shift[None], coarse_bias[None],
        )
    ])
    return pl.pallas_call(
        finish,
        out_shape=(
            jax.ShapeDtypeStruct(features.shape, bf16),
            jax.ShapeDtypeStruct((1, 128, 512), bf16),
        ),
        in_specs=[vmem] * 5,
        out_specs=(hbm, hbm),
        scratch_shapes=[pltpu.VMEM((1, 128, 512), bf16), pltpu.SemaphoreType.DMA((2,))],
        compiler_params=pltpu.CompilerParams(vmem_limit_bytes=16 * 1024 * 1024),
        name="finish",
    )(*found)


def solution(mesh):
    wide = P(AXES, None, None)
    return jax.shard_map(
        shards,
        mesh=mesh,
        in_specs=(wide, P(AXES, None), P(AXES, None), P(AXES), P(), P(), P(), P(), P()),
        out_specs=(wide, wide),
        check_vma=False,
    )
```

```python
import jax
import jax.numpy as jnp
import numpy as np
from jax import lax
from jax.experimental import pallas as pl
from jax.experimental.pallas import tpu as pltpu
from jax.sharding import PartitionSpec as P

norm_eps = 1e-06
AXES = ("bricks", "grp")


def stride_matrix():
    table = np.zeros((512, 512), np.float32)
    for x in range(8):
        for y in range(8):
            for z in range(8):
                tap = 4 * (x % 2) + 2 * (y % 2) + z % 2
                place = 16 * (x // 2) + 4 * (y // 2) + z // 2
                table[64 * x + 8 * y + z, 64 * tap + place] = 1.0
    return table.astype(jnp.bfloat16)


def column(row):
    n = row.shape[1]
    at = lax.broadcasted_iota(jnp.int32, (n, n), 0)
    to = lax.broadcasted_iota(jnp.int32, (n, n), 1)
    return jnp.sum(jnp.where(at == to, row, 0.0), axis=1, keepdims=True)


def offset(dx, dy, dz):
    o = 9 * (dx + 1) + 3 * (dy + 1) + dz + 1
    return o - 1 if o > 13 else o


def dot(a, b):
    return jnp.dot(a, b, preferred_element_type=jnp.float32)


def halos(fetch, y_low, z_low):
    halo_y = jnp.where(y_low, fetch(1, 0), fetch(-1, 0))
    halo_z = jnp.where(z_low, fetch(0, 1), fetch(0, -1))
    near = jnp.where(z_low, fetch(1, 1), fetch(1, -1))
    far = jnp.where(z_low, fetch(-1, 1), fetch(-1, -1))
    return halo_y, halo_z, jnp.where(y_low, near, far)


def turn(x, by):
    return pltpu.roll(x, by % 128, 1)


def flipped(x):
    n = x.shape[1]
    at = lax.broadcasted_iota(jnp.int32, (n, n), 0)
    to = lax.broadcasted_iota(jnp.int32, (n, n), 1)
    eye = jnp.where(at == to, 1.0, 0.0).astype(jnp.bfloat16)
    dims = (((1,), (1,)), ((), ()))
    return lax.dot_general(eye, x, dims, preferred_element_type=jnp.float32).astype(jnp.bfloat16)


def stack(own, halo_y, halo_z, corner, ends):
    y_first, y_last, z_first, z_last = ends

    def along_y(x, halo):
        far = turn(halo, 64)
        return (
            turn(jnp.where(y_last, far, x), 8), x, turn(jnp.where(y_first, far, x), -8),
        )

    order = []
    for plane, rim in zip(along_y(own, halo_y), along_y(halo_z, corner)):
        order.append(turn(jnp.where(z_last, turn(rim, -8), plane), 1))
        order.append(plane)
        order.append(turn(jnp.where(z_first, turn(rim, 8), plane), -1))
    return jnp.concatenate(order, axis=0)


def place(keys, near, far, coarse, count):
    k = lax.broadcasted_iota(jnp.int32, (64, 512), 0)
    lane = lax.broadcasted_iota(jnp.int32, (64, 512), 1)
    rest = lane - (64 * (k >> 4) + 8 * ((k >> 2) & 3) + (k & 3))
    o = keys & 7
    starts = 256 * (o >> 2) + 32 * ((o >> 1) & 1) + 4 * (o & 1)
    starts = jnp.where((keys >> 3) == coarse, starts, -1024)
    starts = jnp.concatenate([starts] * 4, axis=1)
    blocks = [
        jnp.where(rest == starts[j : j + 1], 1.0, 0.0).astype(jnp.bfloat16) for j in range(count)
    ]
    octants = jnp.concatenate([near, far], axis=1)
    return dot(octants, jnp.concatenate(blocks, axis=0))


def kernel(
    occ_hbm, gain_hbm, feat_hbm, map_hbm, near_hbm, weight_hbm, perm_hbm,
    stride_hbm, shift_hbm, bias_hbm,
    fine, keys, keys_in, octs, octs_in,
    occ_ref, gain_ref, feat, map_ref, near_ref, weight, perm,
    stride, shift_ref, bias_ref,
    act, lower, upper, conv, weight_t, rising, falling, risen, fallen,
    local_sem, send_sem, recv_sem,
):
    count = feat.shape[0]
    groups = lax.axis_size("grp")
    peers = groups * lax.axis_size("bricks")
    device = lax.axis_index("bricks") * groups + lax.axis_index("grp")
    has_left = device > 0
    has_right = device < peers - 1

    def coords(other):
        return {"bricks": other // groups, "grp": other % groups}

    loads = [
        pltpu.make_async_copy(src, dst, local_sem.at[n])
        for n, (src, dst) in enumerate(
            [
                (occ_hbm, occ_ref), (gain_hbm, gain_ref),
                (feat_hbm.at[:, :, pl.ds(0, 128)], feat.at[:, :, pl.ds(0, 128)]),
                (feat_hbm.at[:, :, pl.ds(384, 128)], feat.at[:, :, pl.ds(384, 128)]),
                (map_hbm, map_ref), (weight_hbm, weight),
                (feat_hbm.at[:, :, pl.ds(128, 256)], feat.at[:, :, pl.ds(128, 256)]),
                (near_hbm, near_ref), (perm_hbm, perm),
                (stride_hbm, stride), (shift_hbm, shift_ref), (bias_hbm, bias_ref),
            ]
        )
    ]
    for load in loads:
        load.start()
    barrier = pltpu.get_barrier_semaphore()

    @pl.when(has_left)
    def _():
        pl.semaphore_signal(
            barrier, inc=1, device_id=coords(device - 1), device_id_type=pl.DeviceIdType.MESH
        )

    @pl.when(has_right)
    def _():
        pl.semaphore_signal(
            barrier, inc=1, device_id=coords(device + 1), device_id_type=pl.DeviceIdType.MESH
        )

    act[count] = jnp.zeros((64, 512), jnp.bfloat16)
    lower[count] = jnp.zeros((64, 128), jnp.bfloat16)
    upper[count] = jnp.zeros((64, 128), jnp.bfloat16)

    @pl.when(jnp.logical_not(has_left))
    def _():
        risen[...] = jnp.zeros(risen.shape, jnp.bfloat16)

    @pl.when(jnp.logical_not(has_right))
    def _():
        fallen[...] = jnp.zeros(fallen.shape, jnp.bfloat16)

    for load in loads[:4]:
        load.wait()
    gain = column(gain_ref[...])
    lane = lax.broadcasted_iota(jnp.int32, (64, 128), 1)
    half = lane < 64

    def activate(i, start, size):
        lanes = slice(start, start + size)
        values = feat[i, :, lanes].astype(jnp.float32)
        scale = lax.rsqrt(jnp.mean(values * values, axis=0, keepdims=True) + norm_eps)
        normed = values * scale * gain
        mask = occ_ref[pl.ds(i, 1), lanes].astype(jnp.float32)
        result = (normed * (mask * 0.5) * (1.0 + jnp.tanh(0.5 * normed))).astype(jnp.bfloat16)
        act[i, :, lanes] = result
        return result

    for j in range(count // 2):
        left, right = activate(2 * j, 0, 128), activate(2 * j + 1, 0, 128)
        falling[j] = jnp.where(half, left, turn(right, 64))
        left, right = activate(2 * j, 384, 128), activate(2 * j + 1, 384, 128)
        rising[j] = jnp.where(half, turn(left, 64), right)

    def remote(n, src, dst, other):
        return pltpu.make_async_remote_copy(
            src_ref=src, dst_ref=dst, send_sem=send_sem.at[n], recv_sem=recv_sem.at[n],
            device_id=coords(other), device_id_type=pl.DeviceIdType.MESH,
        )

    rise = remote(0, rising, risen, device + 1)
    fall = remote(1, falling, fallen, device - 1)
    mate = device + 1 - 2 * (device % 2)
    swap_keys = remote(2, keys, keys_in, mate)

    pl.semaphore_wait(barrier, has_left.astype(jnp.int32) + has_right.astype(jnp.int32))

    @pl.when(has_right)
    def _():
        rise.start()

    @pl.when(has_left)
    def _():
        fall.start()

    loads[4].wait()
    keys[...] = jnp.broadcast_to(
        column(map_ref[...].astype(jnp.float32)).astype(jnp.int32), keys.shape
    )
    swap_keys.start()

    for load in loads[5:]:
        load.wait()
    shift = column(shift_ref[...])
    bias = column(bias_ref[...])
    stride_t = flipped(stride[...])
    for a in range(3):
        weight_t[64 * a : 64 * a + 64] = flipped(weight[576 * a : 576 * a + 576])

    def activate_rest(i, carry):
        activate(i, 128, 256)
        return carry

    lax.fori_loop(0, count, activate_rest, 0, unroll=4)
    y_low = (lane & 63) < 32
    z_low = (lane & 7) < 4
    marks = ((lane & 63) < 8, (lane & 63) >= 56, (lane & 7) == 0, (lane & 7) == 7)

    def row(i, dx, dy, dz):
        target = near_ref[i, offset(dx, dy, dz)]
        local = jnp.clip(target - (device + dx) * count, 0, count - 1)
        return jnp.where(target < 0, count, local)

    def middle(i, carry):
        rows = {
            (dy, dz): row(i, 0, dy, dz)
            for dy in (-1, 0, 1) for dz in (-1, 0, 1) if (dy, dz) != (0, 0)
        }
        columns = []
        for p in range(4):

            def own(dy, dz):
                return act[rows[dy, dz], :, 128 * p : 128 * p + 128]

            tile = act[i, :, 128 * p : 128 * p + 128]
            columns.append(stack(tile, *halos(own, y_low, z_low), marks))
        product = dot(weight_t[...], jnp.concatenate(columns, axis=1))

        def part(dx, p):
            if not 0 <= p < 4:
                return jnp.zeros((64, 128), jnp.float32)
            return product[64 * (dx + 1) : 64 * (dx + 2), 128 * p : 128 * p + 128]

        pieces = []
        for p in range(4):
            below = pltpu.roll(jnp.where(half, part(-1, p), part(-1, p - 1)), 64, 1)
            above = pltpu.roll(jnp.where(half, part(1, p + 1), part(1, p)), 64, 1)
            pieces.append(part(0, p) + below + above)
        conv[i] = jnp.concatenate(pieces, axis=1)
        return carry

    lax.fori_loop(0, count, middle, 0, unroll=2)

    @pl.when(has_left)
    def _():
        rise.wait_recv()
        fall.wait_send()

    @pl.when(has_right)
    def _():
        fall.wait_recv()
        rise.wait_send()

    for j in range(count // 2):
        lower[2 * j] = turn(risen[j], 64)
        lower[2 * j + 1] = risen[j]
        upper[2 * j] = fallen[j]
        upper[2 * j + 1] = turn(fallen[j], 64)

    step = count // 2
    outside = jnp.concatenate([weight_t[0:64], weight_t[128:192]], axis=0)
    sent = []
    for g in range(2):
        group = pl.ds(g * step, step)
        tall = []
        for n in range(step):
            i = g * step + n

            def outer(dy, dz):
                return jnp.where(half, upper[row(i, 1, dy, dz)], lower[row(i, -1, dy, dz)])

            tall.append(stack(outer(0, 0), *halos(outer, y_low, z_low), marks))
        stacked = jnp.concatenate(tall, axis=1)
        product = dot(outside, stacked)
        for n in range(step):
            i = g * step + n
            mine = product[:, 128 * n : 128 * n + 128]
            turned = pltpu.roll(jnp.where(half, mine[64:], mine[:64]), 64, 1)
            mask = occ_ref[pl.ds(i, 1), :].astype(jnp.float32)
            summed = feat[i].astype(jnp.float32) + conv[i] + shift
            ends = jnp.concatenate(
                [
                    jnp.where(half, turned, 0.0),
                    jnp.zeros((64, 256), jnp.float32),
                    jnp.where(half, 0.0, turned),
                ],
                axis=1,
            )
            fine[i] = (mask * (summed + ends)).astype(jnp.bfloat16)
        ordered = dot(fine[group].reshape(step * 64, 512), perm[...])
        columns = []
        for j in range(0, step, 2):
            taps = []
            for s in range(4):
                one = ordered[64 * j : 64 * j + 64, 128 * s : 128 * s + 128]
                two = ordered[64 * j + 64 : 64 * j + 128, 128 * s : 128 * s + 128]
                taps.append(jnp.where(half, one, pltpu.roll(two, 64, 1)))
                taps.append(jnp.where(half, pltpu.roll(one, 64, 1), two))
            columns.append(jnp.concatenate(taps, axis=0).astype(jnp.bfloat16))
        octants = dot(stride_t, jnp.concatenate(columns, axis=1)) + bias
        octs[g] = octants.astype(jnp.bfloat16)
        swap = remote(3 + g, octs.at[g], octs_in.at[g], mate)
        swap.start()
        sent.append(swap)

    swap_keys.wait()
    for swap in sent:
        swap.wait()


def finish(fine, keys, keys_in, octs, octs_in, fine_hbm, coarse_hbm, coarse, sem):
    count = fine.shape[0]
    device = lax.axis_index("bricks") * lax.axis_size("grp") + lax.axis_index("grp")
    store = pltpu.make_async_copy(fine, fine_hbm, sem.at[0])
    store.start()
    total = place(keys[...], octs[0], octs[1], device, count)
    total = total + place(keys_in[...], octs_in[0], octs_in[1], device, count)
    coarse[0] = total.astype(jnp.bfloat16)
    last = pltpu.make_async_copy(coarse, coarse_hbm, sem.at[1])
    last.start()
    store.wait()
    last.wait()


def shards(
    features, occupancy, neighbours, coarse_map, norm_gain, time_shift, conv_weight,
    stride_weight, coarse_bias,
):
    count = features.shape[0]
    bf16 = jnp.bfloat16
    hbm = pl.BlockSpec(memory_space=pltpu.HBM)
    vmem = pl.BlockSpec(memory_space=pltpu.VMEM)
    found = pl.pallas_call(
        kernel,
        out_shape=(
            jax.ShapeDtypeStruct(features.shape, bf16),
            jax.ShapeDtypeStruct((count, 128), jnp.int32),
            jax.ShapeDtypeStruct((count, 128), jnp.int32),
            jax.ShapeDtypeStruct((2, 128, 32 * count), bf16),
            jax.ShapeDtypeStruct((2, 128, 32 * count), bf16),
        ),
        in_specs=[hbm] * 10,
        out_specs=(vmem,) * 5,
        scratch_shapes=[
            pltpu.VMEM((count, 512), jnp.int32),
            pltpu.VMEM((1, 64), jnp.float32),
            pltpu.VMEM((count, 64, 512), bf16),
            pltpu.VMEM((1, count), jnp.int32),
            pltpu.SMEM((count, 26), jnp.int32),
            pltpu.VMEM((1728, 64), bf16),
            pltpu.VMEM((512, 512), bf16),
            pltpu.VMEM((512, 128), bf16),
            pltpu.VMEM((1, 64), jnp.float32),
            pltpu.VMEM((1, 128), jnp.float32),
            pltpu.VMEM((count + 1, 64, 512), bf16),
            pltpu.VMEM((count + 1, 64, 128), bf16),
            pltpu.VMEM((count + 1, 64, 128), bf16),
            pltpu.VMEM((count, 64, 512), jnp.float32),
            pltpu.VMEM((192, 576), bf16),
            pltpu.VMEM((count // 2, 64, 128), bf16),
            pltpu.VMEM((count // 2, 64, 128), bf16),
            pltpu.VMEM((count // 2, 64, 128), bf16),
            pltpu.VMEM((count // 2, 64, 128), bf16),
            pltpu.SemaphoreType.DMA((16,)),
            pltpu.SemaphoreType.DMA((5,)),
            pltpu.SemaphoreType.DMA((5,)),
        ],
        compiler_params=pltpu.CompilerParams(
            collective_id=0, has_side_effects=True, vmem_limit_bytes=32 * 1024 * 1024
        ),
        name="bricks",
    )(*[
        pltpu.with_memory_space_constraint(x, pltpu.HBM)
        for x in (
            occupancy, norm_gain[None], features, coarse_map[None], neighbours,
            conv_weight.reshape(1728, 64), stride_matrix(),
            stride_weight.reshape(512, 128), time_shift[None], coarse_bias[None],
        )
    ])
    return pl.pallas_call(
        finish,
        out_shape=(
            jax.ShapeDtypeStruct(features.shape, bf16),
            jax.ShapeDtypeStruct((1, 128, 512), bf16),
        ),
        in_specs=[vmem] * 5,
        out_specs=(hbm, hbm),
        scratch_shapes=[pltpu.VMEM((1, 128, 512), bf16), pltpu.SemaphoreType.DMA((2,))],
        compiler_params=pltpu.CompilerParams(vmem_limit_bytes=16 * 1024 * 1024),
        name="finish",
    )(*found)


def solution(mesh):
    wide = P(AXES, None, None)
    return jax.shard_map(
        shards,
        mesh=mesh,
        in_specs=(wide, P(AXES, None), P(AXES, None), P(AXES), P(), P(), P(), P(), P()),
        out_specs=(wide, wide),
        check_vma=False,
    )
```

```python
import jax
import jax.numpy as jnp
import numpy as np
from jax import lax
from jax.experimental import pallas as pl
from jax.experimental.pallas import tpu as pltpu
from jax.sharding import PartitionSpec as P

norm_eps = 1e-06
AXES = ("bricks", "grp")


def side_matrix():
    table = np.zeros((2, 16, 8, 2, 16, 8), np.float32)
    for w, shift in enumerate((-1, 1)):
        for z in range(8):
            kind = 0 if 0 <= z + shift < 8 else 1
            for line in range(16):
                table[kind, line, (z + shift) % 8, w, line, z] = 1.0
    return table.reshape(256, 256).astype(jnp.bfloat16)


def stride_matrix():
    table = np.zeros((512, 512), np.float32)
    for x in range(8):
        for y in range(8):
            for z in range(8):
                tap = 4 * (x % 2) + 2 * (y % 2) + z % 2
                place = 16 * (x // 2) + 4 * (y // 2) + z // 2
                table[64 * x + 8 * y + z, 64 * tap + place] = 1.0
    return table.astype(jnp.bfloat16)


def column(row):
    n = row.shape[1]
    at = lax.broadcasted_iota(jnp.int32, (n, n), 0)
    to = lax.broadcasted_iota(jnp.int32, (n, n), 1)
    return jnp.sum(jnp.where(at == to, row, 0.0), axis=1, keepdims=True)


def offset(dx, dy, dz):
    o = 9 * (dx + 1) + 3 * (dy + 1) + dz + 1
    return o - 1 if o > 13 else o


def dot(a, b):
    return jnp.dot(a, b, preferred_element_type=jnp.float32)


def halos(fetch, y_low, z_low):
    halo_y = jnp.where(y_low, fetch(1, 0), fetch(-1, 0))
    halo_z = jnp.where(z_low, fetch(0, 1), fetch(0, -1))
    near = jnp.where(z_low, fetch(1, 1), fetch(1, -1))
    far = jnp.where(z_low, fetch(-1, 1), fetch(-1, -1))
    return halo_y, halo_z, jnp.where(y_low, near, far)


def turn(x, by):
    return pltpu.roll(x, by % 128, 1)


def flipped(x):
    n = x.shape[1]
    at = lax.broadcasted_iota(jnp.int32, (n, n), 0)
    to = lax.broadcasted_iota(jnp.int32, (n, n), 1)
    eye = jnp.where(at == to, 1.0, 0.0).astype(jnp.bfloat16)
    dims = (((1,), (1,)), ((), ()))
    return lax.dot_general(eye, x, dims, preferred_element_type=jnp.float32).astype(jnp.bfloat16)


def stack(tiles, ends, side):
    y_first, y_last = ends

    def along_y(x, halo):
        far = turn(halo, 64)
        return (
            turn(jnp.where(y_last, far, x), 8), x, turn(jnp.where(y_first, far, x), -8),
        )

    planes = []
    rims = []
    for own, halo_y, halo_z, corner in tiles:
        planes.append(along_y(own, halo_y))
        rims.append(along_y(halo_z, corner))
    pairs = [
        jnp.concatenate([plane[b], rim[b]], axis=1)
        for b in range(3) for plane, rim in zip(planes, rims)
    ]
    moved = dot(jnp.concatenate(pairs, axis=0), side).astype(jnp.bfloat16)
    columns = []
    for t, plane in enumerate(planes):
        order = []
        for b in range(3):
            at = 64 * (b * len(tiles) + t)
            part = moved[at : at + 64]
            order += [part[:, :128], plane[b], part[:, 128:]]
        columns.append(jnp.concatenate(order, axis=0))
    return jnp.concatenate(columns, axis=1)


def place(keys, near, far, coarse, count):
    k = lax.broadcasted_iota(jnp.int32, (64, 512), 0)
    lane = lax.broadcasted_iota(jnp.int32, (64, 512), 1)
    rest = lane - (64 * (k >> 4) + 8 * ((k >> 2) & 3) + (k & 3))
    o = keys & 7
    starts = 256 * (o >> 2) + 32 * ((o >> 1) & 1) + 4 * (o & 1)
    starts = jnp.where((keys >> 3) == coarse, starts, -1024)
    starts = jnp.concatenate([starts] * 4, axis=1)
    blocks = [
        jnp.where(rest == starts[j : j + 1], 1.0, 0.0).astype(jnp.bfloat16) for j in range(count)
    ]
    octants = jnp.concatenate([near, far], axis=1)
    return dot(octants, jnp.concatenate(blocks, axis=0))


def kernel(
    occ_hbm, gain_hbm, feat_hbm, map_hbm, near_hbm, weight_hbm, side_hbm, perm_hbm,
    stride_hbm, shift_hbm, bias_hbm,
    fine, keys, keys_in, octs, octs_in,
    occ_ref, gain_ref, feat, map_ref, near_ref, weight, side, perm,
    stride, shift_ref, bias_ref,
    act, lower, upper, conv, weight_t, rising, falling, risen, fallen,
    local_sem, send_sem, recv_sem,
):
    count = feat.shape[0]
    groups = lax.axis_size("grp")
    peers = groups * lax.axis_size("bricks")
    device = lax.axis_index("bricks") * groups + lax.axis_index("grp")
    has_left = device > 0
    has_right = device < peers - 1

    def coords(other):
        return {"bricks": other // groups, "grp": other % groups}

    loads = [
        pltpu.make_async_copy(src, dst, local_sem.at[n])
        for n, (src, dst) in enumerate(
            [
                (occ_hbm, occ_ref), (gain_hbm, gain_ref),
                (feat_hbm.at[:, :, pl.ds(0, 128)], feat.at[:, :, pl.ds(0, 128)]),
                (feat_hbm.at[:, :, pl.ds(384, 128)], feat.at[:, :, pl.ds(384, 128)]),
                (map_hbm, map_ref), (weight_hbm, weight),
                (feat_hbm.at[:, :, pl.ds(128, 256)], feat.at[:, :, pl.ds(128, 256)]),
                (near_hbm, near_ref), (side_hbm, side), (perm_hbm, perm),
                (stride_hbm, stride), (shift_hbm, shift_ref), (bias_hbm, bias_ref),
            ]
        )
    ]
    for load in loads:
        load.start()
    barrier = pltpu.get_barrier_semaphore()

    @pl.when(has_left)
    def _():
        pl.semaphore_signal(
            barrier, inc=1, device_id=coords(device - 1), device_id_type=pl.DeviceIdType.MESH
        )

    @pl.when(has_right)
    def _():
        pl.semaphore_signal(
            barrier, inc=1, device_id=coords(device + 1), device_id_type=pl.DeviceIdType.MESH
        )

    act[count] = jnp.zeros((64, 512), jnp.bfloat16)
    lower[count] = jnp.zeros((64, 128), jnp.bfloat16)
    upper[count] = jnp.zeros((64, 128), jnp.bfloat16)

    @pl.when(jnp.logical_not(has_left))
    def _():
        risen[...] = jnp.zeros(risen.shape, jnp.bfloat16)

    @pl.when(jnp.logical_not(has_right))
    def _():
        fallen[...] = jnp.zeros(fallen.shape, jnp.bfloat16)

    for load in loads[:4]:
        load.wait()
    gain = column(gain_ref[...])
    lane = lax.broadcasted_iota(jnp.int32, (64, 128), 1)
    half = lane < 64

    def activate(i, start, size):
        lanes = slice(start, start + size)
        values = feat[i, :, lanes].astype(jnp.float32)
        scale = lax.rsqrt(jnp.mean(values * values, axis=0, keepdims=True) + norm_eps)
        normed = values * scale * gain
        mask = occ_ref[pl.ds(i, 1), lanes].astype(jnp.float32)
        result = (normed * (mask * 0.5) * (1.0 + jnp.tanh(0.5 * normed))).astype(jnp.bfloat16)
        act[i, :, lanes] = result
        return result

    for j in range(count // 2):
        left, right = activate(2 * j, 0, 128), activate(2 * j + 1, 0, 128)
        falling[j] = jnp.where(half, left, turn(right, 64))
        left, right = activate(2 * j, 384, 128), activate(2 * j + 1, 384, 128)
        rising[j] = jnp.where(half, turn(left, 64), right)

    def remote(n, src, dst, other):
        return pltpu.make_async_remote_copy(
            src_ref=src, dst_ref=dst, send_sem=send_sem.at[n], recv_sem=recv_sem.at[n],
            device_id=coords(other), device_id_type=pl.DeviceIdType.MESH,
        )

    rise = remote(0, rising, risen, device + 1)
    fall = remote(1, falling, fallen, device - 1)
    mate = device + 1 - 2 * (device % 2)
    swap_keys = remote(2, keys, keys_in, mate)

    pl.semaphore_wait(barrier, has_left.astype(jnp.int32) + has_right.astype(jnp.int32))

    @pl.when(has_right)
    def _():
        rise.start()

    @pl.when(has_left)
    def _():
        fall.start()

    loads[4].wait()
    keys[...] = jnp.broadcast_to(
        column(map_ref[...].astype(jnp.float32)).astype(jnp.int32), keys.shape
    )
    swap_keys.start()

    for load in loads[5:]:
        load.wait()
    shift = column(shift_ref[...])
    bias = column(bias_ref[...])
    stride_t = flipped(stride[...])
    for a in range(3):
        weight_t[64 * a : 64 * a + 64] = flipped(weight[576 * a : 576 * a + 576])

    def activate_rest(i, carry):
        activate(i, 128, 256)
        return carry

    lax.fori_loop(0, count, activate_rest, 0, unroll=4)
    y_low = (lane & 63) < 32
    z_low = (lane & 7) < 4
    marks = ((lane & 63) < 8, (lane & 63) >= 56)

    def row(i, dx, dy, dz):
        target = near_ref[i, offset(dx, dy, dz)]
        local = jnp.clip(target - (device + dx) * count, 0, count - 1)
        return jnp.where(target < 0, count, local)

    def middle(i, carry):
        rows = {
            (dy, dz): row(i, 0, dy, dz)
            for dy in (-1, 0, 1) for dz in (-1, 0, 1) if (dy, dz) != (0, 0)
        }
        columns = []
        for p in range(4):

            def own(dy, dz):
                return act[rows[dy, dz], :, 128 * p : 128 * p + 128]

            tile = act[i, :, 128 * p : 128 * p + 128]
            columns.append((tile, *halos(own, y_low, z_low)))
        product = dot(weight_t[...], stack(columns, marks, side[...]))

        def part(dx, p):
            if not 0 <= p < 4:
                return jnp.zeros((64, 128), jnp.float32)
            return product[64 * (dx + 1) : 64 * (dx + 2), 128 * p : 128 * p + 128]

        pieces = []
        for p in range(4):
            below = jnp.where(half, part(-1, p), part(-1, p - 1))
            above = jnp.where(half, part(1, p + 1), part(1, p))
            pieces.append(part(0, p) + turn(below + above, 64))
        conv[i] = jnp.concatenate(pieces, axis=1)
        return carry

    lax.fori_loop(0, count, middle, 0, unroll=4)

    @pl.when(has_left)
    def _():
        rise.wait_recv()
        fall.wait_send()

    @pl.when(has_right)
    def _():
        fall.wait_recv()
        rise.wait_send()

    for j in range(count // 2):
        lower[2 * j] = turn(risen[j], 64)
        lower[2 * j + 1] = risen[j]
        upper[2 * j] = fallen[j]
        upper[2 * j + 1] = turn(fallen[j], 64)

    step = count // 2
    outside = jnp.concatenate([weight_t[0:64], weight_t[128:192]], axis=0)
    sent = []
    for g in range(2):
        group = pl.ds(g * step, step)
        tall = []
        for n in range(step):
            i = g * step + n

            def outer(dy, dz):
                return jnp.where(half, upper[row(i, 1, dy, dz)], lower[row(i, -1, dy, dz)])

            tall.append((outer(0, 0), *halos(outer, y_low, z_low)))
        stacked = stack(tall, marks, side[...])
        product = dot(outside, stacked)
        for n in range(step):
            i = g * step + n
            mine = product[:, 128 * n : 128 * n + 128]
            turned = pltpu.roll(jnp.where(half, mine[64:], mine[:64]), 64, 1)
            mask = occ_ref[pl.ds(i, 1), :].astype(jnp.float32)
            summed = feat[i].astype(jnp.float32) + conv[i] + shift
            ends = jnp.concatenate(
                [
                    jnp.where(half, turned, 0.0),
                    jnp.zeros((64, 256), jnp.float32),
                    jnp.where(half, 0.0, turned),
                ],
                axis=1,
            )
            fine[i] = (mask * (summed + ends)).astype(jnp.bfloat16)
        ordered = dot(fine[group].reshape(step * 64, 512), perm[...])
        columns = []
        for j in range(0, step, 2):
            taps = []
            for s in range(4):
                one = ordered[64 * j : 64 * j + 64, 128 * s : 128 * s + 128]
                two = ordered[64 * j + 64 : 64 * j + 128, 128 * s : 128 * s + 128]
                taps.append(jnp.where(half, one, pltpu.roll(two, 64, 1)))
                taps.append(jnp.where(half, pltpu.roll(one, 64, 1), two))
            columns.append(jnp.concatenate(taps, axis=0).astype(jnp.bfloat16))
        octants = dot(stride_t, jnp.concatenate(columns, axis=1)) + bias
        octs[g] = octants.astype(jnp.bfloat16)
        swap = remote(3 + g, octs.at[g], octs_in.at[g], mate)
        swap.start()
        sent.append(swap)

    swap_keys.wait()
    for swap in sent:
        swap.wait()


def finish(fine, keys, keys_in, octs, octs_in, fine_hbm, coarse_hbm, coarse, sem):
    count = fine.shape[0]
    device = lax.axis_index("bricks") * lax.axis_size("grp") + lax.axis_index("grp")
    store = pltpu.make_async_copy(fine, fine_hbm, sem.at[0])
    store.start()
    total = place(keys[...], octs[0], octs[1], device, count)
    total = total + place(keys_in[...], octs_in[0], octs_in[1], device, count)
    coarse[0] = total.astype(jnp.bfloat16)
    last = pltpu.make_async_copy(coarse, coarse_hbm, sem.at[1])
    last.start()
    store.wait()
    last.wait()


def shards(
    features, occupancy, neighbours, coarse_map, norm_gain, time_shift, conv_weight,
    stride_weight, coarse_bias,
):
    count = features.shape[0]
    bf16 = jnp.bfloat16
    hbm = pl.BlockSpec(memory_space=pltpu.HBM)
    vmem = pl.BlockSpec(memory_space=pltpu.VMEM)
    found = pl.pallas_call(
        kernel,
        out_shape=(
            jax.ShapeDtypeStruct(features.shape, bf16),
            jax.ShapeDtypeStruct((count, 128), jnp.int32),
            jax.ShapeDtypeStruct((count, 128), jnp.int32),
            jax.ShapeDtypeStruct((2, 128, 32 * count), bf16),
            jax.ShapeDtypeStruct((2, 128, 32 * count), bf16),
        ),
        in_specs=[hbm] * 11,
        out_specs=(vmem,) * 5,
        scratch_shapes=[
            pltpu.VMEM((count, 512), jnp.int32),
            pltpu.VMEM((1, 64), jnp.float32),
            pltpu.VMEM((count, 64, 512), bf16),
            pltpu.VMEM((1, count), jnp.int32),
            pltpu.SMEM((count, 26), jnp.int32),
            pltpu.VMEM((1728, 64), bf16),
            pltpu.VMEM((256, 256), bf16),
            pltpu.VMEM((512, 512), bf16),
            pltpu.VMEM((512, 128), bf16),
            pltpu.VMEM((1, 64), jnp.float32),
            pltpu.VMEM((1, 128), jnp.float32),
            pltpu.VMEM((count + 1, 64, 512), bf16),
            pltpu.VMEM((count + 1, 64, 128), bf16),
            pltpu.VMEM((count + 1, 64, 128), bf16),
            pltpu.VMEM((count, 64, 512), jnp.float32),
            pltpu.VMEM((192, 576), bf16),
            pltpu.VMEM((count // 2, 64, 128), bf16),
            pltpu.VMEM((count // 2, 64, 128), bf16),
            pltpu.VMEM((count // 2, 64, 128), bf16),
            pltpu.VMEM((count // 2, 64, 128), bf16),
            pltpu.SemaphoreType.DMA((16,)),
            pltpu.SemaphoreType.DMA((5,)),
            pltpu.SemaphoreType.DMA((5,)),
        ],
        compiler_params=pltpu.CompilerParams(
            collective_id=0, has_side_effects=True, vmem_limit_bytes=32 * 1024 * 1024
        ),
        name="bricks",
    )(*[
        pltpu.with_memory_space_constraint(x, pltpu.HBM)
        for x in (
            occupancy, norm_gain[None], features, coarse_map[None], neighbours,
            conv_weight.reshape(1728, 64), side_matrix(), stride_matrix(),
            stride_weight.reshape(512, 128), time_shift[None], coarse_bias[None],
        )
    ])
    return pl.pallas_call(
        finish,
        out_shape=(
            jax.ShapeDtypeStruct(features.shape, bf16),
            jax.ShapeDtypeStruct((1, 128, 512), bf16),
        ),
        in_specs=[vmem] * 5,
        out_specs=(hbm, hbm),
        scratch_shapes=[pltpu.VMEM((1, 128, 512), bf16), pltpu.SemaphoreType.DMA((2,))],
        compiler_params=pltpu.CompilerParams(vmem_limit_bytes=16 * 1024 * 1024),
        name="finish",
    )(*found)


def solution(mesh):
    wide = P(AXES, None, None)
    return jax.shard_map(
        shards,
        mesh=mesh,
        in_specs=(wide, P(AXES, None), P(AXES, None), P(AXES), P(), P(), P(), P(), P()),
        out_specs=(wide, wide),
        check_vma=False,
    )
```

```python
import jax
import jax.numpy as jnp
import numpy as np
from jax import lax
from jax.experimental import pallas as pl
from jax.experimental.pallas import tpu as pltpu
from jax.sharding import PartitionSpec as P

norm_eps = 1e-06
AXES = ("bricks", "grp")


def side_matrix():
    table = np.zeros((2, 16, 8, 2, 16, 8), np.float32)
    for w, shift in enumerate((-1, 1)):
        for z in range(8):
            kind = 0 if 0 <= z + shift < 8 else 1
            for line in range(16):
                table[kind, line, (z + shift) % 8, w, line, z] = 1.0
    return table.reshape(256, 256).astype(jnp.bfloat16)


def stride_matrix():
    table = np.zeros((512, 512), np.float32)
    for x in range(8):
        for y in range(8):
            for z in range(8):
                tap = 4 * (x % 2) + 2 * (y % 2) + z % 2
                place = 16 * (x // 2) + 4 * (y // 2) + z // 2
                table[64 * x + 8 * y + z, 64 * tap + place] = 1.0
    return table.astype(jnp.bfloat16)


def column(row):
    n = row.shape[1]
    at = lax.broadcasted_iota(jnp.int32, (n, n), 0)
    to = lax.broadcasted_iota(jnp.int32, (n, n), 1)
    return jnp.sum(jnp.where(at == to, row, 0.0), axis=1, keepdims=True)


def offset(dx, dy, dz):
    o = 9 * (dx + 1) + 3 * (dy + 1) + dz + 1
    return o - 1 if o > 13 else o


def dot(a, b):
    return jnp.dot(a, b, preferred_element_type=jnp.float32)


def halos(fetch, y_low, z_low):
    halo_y = jnp.where(y_low, fetch(1, 0), fetch(-1, 0))
    halo_z = jnp.where(z_low, fetch(0, 1), fetch(0, -1))
    near = jnp.where(z_low, fetch(1, 1), fetch(1, -1))
    far = jnp.where(z_low, fetch(-1, 1), fetch(-1, -1))
    return halo_y, halo_z, jnp.where(y_low, near, far)


def turn(x, by):
    return pltpu.roll(x, by % 128, 1)


def flipped(x):
    n = x.shape[1]
    at = lax.broadcasted_iota(jnp.int32, (n, n), 0)
    to = lax.broadcasted_iota(jnp.int32, (n, n), 1)
    eye = jnp.where(at == to, 1.0, 0.0).astype(jnp.bfloat16)
    dims = (((1,), (1,)), ((), ()))
    return lax.dot_general(eye, x, dims, preferred_element_type=jnp.float32).astype(jnp.bfloat16)


def stack(tiles, ends, side):
    y_first, y_last = ends

    def along_y(x, halo):
        far = turn(halo, 64)
        return (
            turn(jnp.where(y_last, far, x), 8), x, turn(jnp.where(y_first, far, x), -8),
        )

    planes = []
    rims = []
    for own, halo_y, halo_z, corner in tiles:
        planes.append(along_y(own, halo_y))
        rims.append(along_y(halo_z, corner))
    pairs = [
        jnp.concatenate([plane[b], rim[b]], axis=1)
        for b in range(3) for plane, rim in zip(planes, rims)
    ]
    moved = dot(jnp.concatenate(pairs, axis=0), side).astype(jnp.bfloat16)
    columns = []
    for t, plane in enumerate(planes):
        order = []
        for b in range(3):
            at = 64 * (b * len(tiles) + t)
            part = moved[at : at + 64]
            order += [part[:, :128], plane[b], part[:, 128:]]
        columns.append(jnp.concatenate(order, axis=0))
    return jnp.concatenate(columns, axis=1)


def place(keys, octants, coarse, count):
    k = lax.broadcasted_iota(jnp.int32, (64, 512), 0)
    lane = lax.broadcasted_iota(jnp.int32, (64, 512), 1)
    rest = lane - (64 * (k >> 4) + 8 * ((k >> 2) & 3) + (k & 3))
    o = keys & 7
    starts = 256 * (o >> 2) + 32 * ((o >> 1) & 1) + 4 * (o & 1)
    starts = jnp.where((keys >> 3) == coarse, starts, -1024)
    starts = jnp.concatenate([starts] * 4, axis=1)
    blocks = [
        jnp.where(rest == starts[j : j + 1], 1.0, 0.0).astype(jnp.bfloat16) for j in range(count)
    ]
    return dot(octants, jnp.concatenate(blocks, axis=0))


def kernel(
    occ_hbm, gain_hbm, feat_hbm, map_hbm, near_hbm, weight_hbm, side_hbm, perm_hbm,
    stride_hbm, shift_hbm, bias_hbm,
    fine, keys, keys_in, octs, octs_in,
    occ_ref, gain_ref, feat, map_ref, near_ref, weight, side, perm,
    stride, shift_ref, bias_ref,
    act, lower, upper, conv, weight_t, rising, falling, risen, fallen,
    local_sem, send_sem, recv_sem,
):
    count = feat.shape[0]
    groups = lax.axis_size("grp")
    peers = groups * lax.axis_size("bricks")
    device = lax.axis_index("bricks") * groups + lax.axis_index("grp")
    has_left = device > 0
    has_right = device < peers - 1

    def coords(other):
        return {"bricks": other // groups, "grp": other % groups}

    loads = [
        pltpu.make_async_copy(src, dst, local_sem.at[n])
        for n, (src, dst) in enumerate(
            [
                (occ_hbm, occ_ref), (gain_hbm, gain_ref),
                (feat_hbm.at[:, :, pl.ds(0, 128)], feat.at[:, :, pl.ds(0, 128)]),
                (feat_hbm.at[:, :, pl.ds(384, 128)], feat.at[:, :, pl.ds(384, 128)]),
                (map_hbm, map_ref), (weight_hbm, weight),
                (feat_hbm.at[:, :, pl.ds(128, 256)], feat.at[:, :, pl.ds(128, 256)]),
                (near_hbm, near_ref), (side_hbm, side), (perm_hbm, perm),
                (stride_hbm, stride), (shift_hbm, shift_ref), (bias_hbm, bias_ref),
            ]
        )
    ]
    for load in loads:
        load.start()
    barrier = pltpu.get_barrier_semaphore()

    @pl.when(has_left)
    def _():
        pl.semaphore_signal(
            barrier, inc=1, device_id=coords(device - 1), device_id_type=pl.DeviceIdType.MESH
        )

    @pl.when(has_right)
    def _():
        pl.semaphore_signal(
            barrier, inc=1, device_id=coords(device + 1), device_id_type=pl.DeviceIdType.MESH
        )

    act[count] = jnp.zeros((64, 512), jnp.bfloat16)
    lower[count] = jnp.zeros((64, 128), jnp.bfloat16)
    upper[count] = jnp.zeros((64, 128), jnp.bfloat16)

    @pl.when(jnp.logical_not(has_left))
    def _():
        risen[...] = jnp.zeros(risen.shape, jnp.bfloat16)

    @pl.when(jnp.logical_not(has_right))
    def _():
        fallen[...] = jnp.zeros(fallen.shape, jnp.bfloat16)

    for load in loads[:4]:
        load.wait()
    gain = column(gain_ref[...])
    lane = lax.broadcasted_iota(jnp.int32, (64, 128), 1)
    half = lane < 64

    def activate(i, start, size):
        lanes = slice(start, start + size)
        values = feat[i, :, lanes].astype(jnp.float32)
        scale = lax.rsqrt(jnp.mean(values * values, axis=0, keepdims=True) + norm_eps)
        normed = values * scale * gain
        mask = occ_ref[pl.ds(i, 1), lanes].astype(jnp.float32)
        result = (normed * (mask * 0.5) * (1.0 + jnp.tanh(0.5 * normed))).astype(jnp.bfloat16)
        act[i, :, lanes] = result
        return result

    for j in range(count // 2):
        left, right = activate(2 * j, 0, 128), activate(2 * j + 1, 0, 128)
        falling[j] = jnp.where(half, left, turn(right, 64))
        left, right = activate(2 * j, 384, 128), activate(2 * j + 1, 384, 128)
        rising[j] = jnp.where(half, turn(left, 64), right)

    def remote(n, src, dst, other):
        return pltpu.make_async_remote_copy(
            src_ref=src, dst_ref=dst, send_sem=send_sem.at[n], recv_sem=recv_sem.at[n],
            device_id=coords(other), device_id_type=pl.DeviceIdType.MESH,
        )

    rise = remote(0, rising, risen, device + 1)
    fall = remote(1, falling, fallen, device - 1)
    mate = device + 1 - 2 * (device % 2)
    swap_keys = remote(2, keys, keys_in, mate)

    pl.semaphore_wait(barrier, has_left.astype(jnp.int32) + has_right.astype(jnp.int32))

    @pl.when(has_right)
    def _():
        rise.start()

    @pl.when(has_left)
    def _():
        fall.start()

    loads[4].wait()
    keys[...] = jnp.broadcast_to(
        column(map_ref[...].astype(jnp.float32)).astype(jnp.int32), keys.shape
    )
    swap_keys.start()

    for load in loads[5:]:
        load.wait()
    shift = column(shift_ref[...])
    bias = column(bias_ref[...])
    stride_t = flipped(stride[...])
    for a in range(3):
        weight_t[64 * a : 64 * a + 64] = flipped(weight[576 * a : 576 * a + 576])

    for i in range(count):
        activate(i, 128, 256)
    y_low = (lane & 63) < 32
    z_low = (lane & 7) < 4
    marks = ((lane & 63) < 8, (lane & 63) >= 56)

    def row(i, dx, dy, dz):
        target = near_ref[i, offset(dx, dy, dz)]
        local = jnp.clip(target - (device + dx) * count, 0, count - 1)
        return jnp.where(target < 0, count, local)

    def middle(i, carry):
        rows = {
            (dy, dz): row(i, 0, dy, dz)
            for dy in (-1, 0, 1) for dz in (-1, 0, 1) if (dy, dz) != (0, 0)
        }
        columns = []
        for p in range(4):

            def own(dy, dz):
                return act[rows[dy, dz], :, 128 * p : 128 * p + 128]

            tile = act[i, :, 128 * p : 128 * p + 128]
            columns.append((tile, *halos(own, y_low, z_low)))
        product = dot(weight_t[...], stack(columns, marks, side[...]))

        def part(dx, p):
            if not 0 <= p < 4:
                return jnp.zeros((64, 128), jnp.float32)
            return product[64 * (dx + 1) : 64 * (dx + 2), 128 * p : 128 * p + 128]

        pieces = []
        for p in range(4):
            below = jnp.where(half, part(-1, p), part(-1, p - 1))
            above = jnp.where(half, part(1, p + 1), part(1, p))
            pieces.append(part(0, p) + turn(below + above, 64))
        conv[i] = jnp.concatenate(pieces, axis=1)
        return carry

    lax.fori_loop(0, count, middle, 0, unroll=4)

    @pl.when(has_left)
    def _():
        rise.wait_recv()
        fall.wait_send()

    @pl.when(has_right)
    def _():
        fall.wait_recv()
        rise.wait_send()

    for j in range(count // 2):
        lower[2 * j] = turn(risen[j], 64)
        lower[2 * j + 1] = risen[j]
        upper[2 * j] = fallen[j]
        upper[2 * j + 1] = turn(fallen[j], 64)

    outside = jnp.concatenate([weight_t[0:64], weight_t[128:192]], axis=0)
    tall = []
    for i in range(count):

        def outer(dy, dz):
            return jnp.where(half, upper[row(i, 1, dy, dz)], lower[row(i, -1, dy, dz)])

        tall.append((outer(0, 0), *halos(outer, y_low, z_low)))
    stacked = stack(tall, marks, side[...])
    product = dot(outside, stacked)
    for i in range(count):
        mine = product[:, 128 * i : 128 * i + 128]
        turned = pltpu.roll(jnp.where(half, mine[64:], mine[:64]), 64, 1)
        mask = occ_ref[pl.ds(i, 1), :].astype(jnp.float32)
        summed = feat[i].astype(jnp.float32) + conv[i] + shift
        ends = jnp.concatenate(
            [
                jnp.where(half, turned, 0.0),
                jnp.zeros((64, 256), jnp.float32),
                jnp.where(half, 0.0, turned),
            ],
            axis=1,
        )
        fine[i] = (mask * (summed + ends)).astype(jnp.bfloat16)
    ordered = dot(fine[...].reshape(count * 64, 512), perm[...])
    columns = []
    for j in range(0, count, 2):
        taps = []
        for s in range(4):
            one = ordered[64 * j : 64 * j + 64, 128 * s : 128 * s + 128]
            two = ordered[64 * j + 64 : 64 * j + 128, 128 * s : 128 * s + 128]
            taps.append(jnp.where(half, one, pltpu.roll(two, 64, 1)))
            taps.append(jnp.where(half, pltpu.roll(one, 64, 1), two))
        columns.append(jnp.concatenate(taps, axis=0).astype(jnp.bfloat16))
    octants = dot(stride_t, jnp.concatenate(columns, axis=1)) + bias
    octs[...] = octants.astype(jnp.bfloat16)
    swap = remote(3, octs, octs_in, mate)
    swap.start()

    swap_keys.wait()
    swap.wait()


def finish(fine, keys, keys_in, octs, octs_in, fine_hbm, coarse_hbm, coarse, sem):
    count = fine.shape[0]
    device = lax.axis_index("bricks") * lax.axis_size("grp") + lax.axis_index("grp")
    store = pltpu.make_async_copy(fine, fine_hbm, sem.at[0])
    store.start()
    total = place(keys[...], octs[...], device, count)
    total = total + place(keys_in[...], octs_in[...], device, count)
    coarse[0] = total.astype(jnp.bfloat16)
    last = pltpu.make_async_copy(coarse, coarse_hbm, sem.at[1])
    last.start()
    store.wait()
    last.wait()


def shards(
    features, occupancy, neighbours, coarse_map, norm_gain, time_shift, conv_weight,
    stride_weight, coarse_bias,
):
    count = features.shape[0]
    bf16 = jnp.bfloat16
    hbm = pl.BlockSpec(memory_space=pltpu.HBM)
    vmem = pl.BlockSpec(memory_space=pltpu.VMEM)
    found = pl.pallas_call(
        kernel,
        out_shape=(
            jax.ShapeDtypeStruct(features.shape, bf16),
            jax.ShapeDtypeStruct((count, 128), jnp.int32),
            jax.ShapeDtypeStruct((count, 128), jnp.int32),
            jax.ShapeDtypeStruct((128, 64 * count), bf16),
            jax.ShapeDtypeStruct((128, 64 * count), bf16),
        ),
        in_specs=[hbm] * 11,
        out_specs=(vmem,) * 5,
        scratch_shapes=[
            pltpu.VMEM((count, 512), jnp.int32),
            pltpu.VMEM((1, 64), jnp.float32),
            pltpu.VMEM((count, 64, 512), bf16),
            pltpu.VMEM((1, count), jnp.int32),
            pltpu.SMEM((count, 26), jnp.int32),
            pltpu.VMEM((1728, 64), bf16),
            pltpu.VMEM((256, 256), bf16),
            pltpu.VMEM((512, 512), bf16),
            pltpu.VMEM((512, 128), bf16),
            pltpu.VMEM((1, 64), jnp.float32),
            pltpu.VMEM((1, 128), jnp.float32),
            pltpu.VMEM((count + 1, 64, 512), bf16),
            pltpu.VMEM((count + 1, 64, 128), bf16),
            pltpu.VMEM((count + 1, 64, 128), bf16),
            pltpu.VMEM((count, 64, 512), jnp.float32),
            pltpu.VMEM((192, 576), bf16),
            pltpu.VMEM((count // 2, 64, 128), bf16),
            pltpu.VMEM((count // 2, 64, 128), bf16),
            pltpu.VMEM((count // 2, 64, 128), bf16),
            pltpu.VMEM((count // 2, 64, 128), bf16),
            pltpu.SemaphoreType.DMA((16,)),
            pltpu.SemaphoreType.DMA((5,)),
            pltpu.SemaphoreType.DMA((5,)),
        ],
        compiler_params=pltpu.CompilerParams(
            collective_id=0, has_side_effects=True, vmem_limit_bytes=32 * 1024 * 1024
        ),
        name="bricks",
    )(*[
        pltpu.with_memory_space_constraint(x, pltpu.HBM)
        for x in (
            occupancy, norm_gain[None], features, coarse_map[None], neighbours,
            conv_weight.reshape(1728, 64), side_matrix(), stride_matrix(),
            stride_weight.reshape(512, 128), time_shift[None], coarse_bias[None],
        )
    ])
    return pl.pallas_call(
        finish,
        out_shape=(
            jax.ShapeDtypeStruct(features.shape, bf16),
            jax.ShapeDtypeStruct((1, 128, 512), bf16),
        ),
        in_specs=[vmem] * 5,
        out_specs=(hbm, hbm),
        scratch_shapes=[pltpu.VMEM((1, 128, 512), bf16), pltpu.SemaphoreType.DMA((2,))],
        compiler_params=pltpu.CompilerParams(vmem_limit_bytes=16 * 1024 * 1024),
        name="finish",
    )(*found)


def solution(mesh):
    wide = P(AXES, None, None)
    return jax.shard_map(
        shards,
        mesh=mesh,
        in_specs=(wide, P(AXES, None), P(AXES, None), P(AXES), P(), P(), P(), P(), P()),
        out_specs=(wide, wide),
        check_vma=False,
    )
```

```python
import jax
import jax.numpy as jnp
import numpy as np
from jax import lax
from jax.experimental import pallas as pl
from jax.experimental.pallas import tpu as pltpu
from jax.sharding import PartitionSpec as P

norm_eps = 1e-06
AXES = ("bricks", "grp")


def side_matrix():
    table = np.zeros((2, 16, 8, 2, 16, 8), np.float32)
    for w, shift in enumerate((-1, 1)):
        for z in range(8):
            kind = 0 if 0 <= z + shift < 8 else 1
            for line in range(16):
                table[kind, line, (z + shift) % 8, w, line, z] = 1.0
    return table.reshape(256, 256).astype(jnp.bfloat16)


def stride_matrix():
    table = np.zeros((512, 512), np.float32)
    for x in range(8):
        for y in range(8):
            for z in range(8):
                tap = 4 * (x % 2) + 2 * (y % 2) + z % 2
                place = 16 * (x // 2) + 4 * (y // 2) + z // 2
                table[64 * x + 8 * y + z, 64 * tap + place] = 1.0
    return table.astype(jnp.bfloat16)


def column(row):
    n = row.shape[1]
    at = lax.broadcasted_iota(jnp.int32, (n, n), 0)
    to = lax.broadcasted_iota(jnp.int32, (n, n), 1)
    return jnp.sum(jnp.where(at == to, row, 0.0), axis=1, keepdims=True)


def offset(dx, dy, dz):
    o = 9 * (dx + 1) + 3 * (dy + 1) + dz + 1
    return o - 1 if o > 13 else o


def dot(a, b):
    return jnp.dot(a, b, preferred_element_type=jnp.float32)


def halos(fetch, y_low, z_low):
    halo_y = jnp.where(y_low, fetch(1, 0), fetch(-1, 0))
    halo_z = jnp.where(z_low, fetch(0, 1), fetch(0, -1))
    near = jnp.where(z_low, fetch(1, 1), fetch(1, -1))
    far = jnp.where(z_low, fetch(-1, 1), fetch(-1, -1))
    return halo_y, halo_z, jnp.where(y_low, near, far)


def turn(x, by):
    return pltpu.roll(x, by % 128, 1)


def flipped(x):
    n = x.shape[1]
    at = lax.broadcasted_iota(jnp.int32, (n, n), 0)
    to = lax.broadcasted_iota(jnp.int32, (n, n), 1)
    eye = jnp.where(at == to, 1.0, 0.0).astype(jnp.bfloat16)
    dims = (((1,), (1,)), ((), ()))
    return lax.dot_general(eye, x, dims, preferred_element_type=jnp.float32).astype(jnp.bfloat16)


def stack(tiles, ends, side):
    y_first, y_last = ends

    def along_y(x, halo):
        far = turn(halo, 64)
        return (
            turn(jnp.where(y_last, far, x), 8), x, turn(jnp.where(y_first, far, x), -8),
        )

    planes = []
    rims = []
    for own, halo_y, halo_z, corner in tiles:
        planes.append(along_y(own, halo_y))
        rims.append(along_y(halo_z, corner))
    pairs = [
        jnp.concatenate([plane[b], rim[b]], axis=1)
        for b in range(3) for plane, rim in zip(planes, rims)
    ]
    moved = dot(jnp.concatenate(pairs, axis=0), side).astype(jnp.bfloat16)
    columns = []
    for t, plane in enumerate(planes):
        order = []
        for b in range(3):
            at = 64 * (b * len(tiles) + t)
            part = moved[at : at + 64]
            order += [part[:, :128], plane[b], part[:, 128:]]
        columns.append(jnp.concatenate(order, axis=0))
    return jnp.concatenate(columns, axis=1)


def place(keys, octants, coarse, count):
    k = lax.broadcasted_iota(jnp.int32, (64, 512), 0)
    lane = lax.broadcasted_iota(jnp.int32, (64, 512), 1)
    rest = lane - (64 * (k >> 4) + 8 * ((k >> 2) & 3) + (k & 3))
    o = keys & 7
    starts = 256 * (o >> 2) + 32 * ((o >> 1) & 1) + 4 * (o & 1)
    starts = jnp.where((keys >> 3) == coarse, starts, -1024)
    starts = jnp.concatenate([starts] * 4, axis=1)
    blocks = [
        jnp.where(rest == starts[j : j + 1], 1.0, 0.0).astype(jnp.bfloat16) for j in range(count)
    ]
    return dot(octants, jnp.concatenate(blocks, axis=0))


def kernel(
    occ_hbm, gain_hbm, feat_hbm, map_hbm, near_hbm, weight_hbm, side_hbm, perm_hbm,
    stride_hbm, shift_hbm, bias_hbm,
    fine, keys, keys_in, octs, octs_in,
    occ_ref, gain_ref, feat, map_ref, near_ref, weight, side, perm,
    stride, shift_ref, bias_ref,
    act, lower, upper, conv, weight_t, rising, falling, risen, fallen,
    local_sem, send_sem, recv_sem,
):
    count = feat.shape[0]
    groups = lax.axis_size("grp")
    peers = groups * lax.axis_size("bricks")
    device = lax.axis_index("bricks") * groups + lax.axis_index("grp")
    has_left = device > 0
    has_right = device < peers - 1

    def coords(other):
        return {"bricks": other // groups, "grp": other % groups}

    loads = [
        pltpu.make_async_copy(src, dst, local_sem.at[n])
        for n, (src, dst) in enumerate(
            [
                (occ_hbm, occ_ref), (gain_hbm, gain_ref),
                (feat_hbm.at[:, :, pl.ds(0, 128)], feat.at[:, :, pl.ds(0, 128)]),
                (feat_hbm.at[:, :, pl.ds(384, 128)], feat.at[:, :, pl.ds(384, 128)]),
                (map_hbm, map_ref), (weight_hbm, weight),
                (feat_hbm.at[:, :, pl.ds(128, 256)], feat.at[:, :, pl.ds(128, 256)]),
                (near_hbm, near_ref), (side_hbm, side), (perm_hbm, perm),
                (stride_hbm, stride), (shift_hbm, shift_ref), (bias_hbm, bias_ref),
            ]
        )
    ]
    for load in loads:
        load.start()
    barrier = pltpu.get_barrier_semaphore()

    @pl.when(has_left)
    def _():
        pl.semaphore_signal(
            barrier, inc=1, device_id=coords(device - 1), device_id_type=pl.DeviceIdType.MESH
        )

    @pl.when(has_right)
    def _():
        pl.semaphore_signal(
            barrier, inc=1, device_id=coords(device + 1), device_id_type=pl.DeviceIdType.MESH
        )

    act[count] = jnp.zeros((64, 512), jnp.bfloat16)
    lower[count] = jnp.zeros((64, 128), jnp.bfloat16)
    upper[count] = jnp.zeros((64, 128), jnp.bfloat16)

    @pl.when(jnp.logical_not(has_left))
    def _():
        risen[...] = jnp.zeros(risen.shape, jnp.bfloat16)

    @pl.when(jnp.logical_not(has_right))
    def _():
        fallen[...] = jnp.zeros(fallen.shape, jnp.bfloat16)

    for load in loads[:4]:
        load.wait()
    gain = column(gain_ref[...])
    lane = lax.broadcasted_iota(jnp.int32, (64, 128), 1)
    half = lane < 64

    def activate(i, start, size):
        lanes = slice(start, start + size)
        values = feat[i, :, lanes].astype(jnp.float32)
        scale = lax.rsqrt(jnp.mean(values * values, axis=0, keepdims=True) + norm_eps)
        normed = values * scale * gain
        mask = occ_ref[pl.ds(i, 1), lanes].astype(jnp.float32)
        result = (normed * (mask * 0.5) * (1.0 + jnp.tanh(0.5 * normed))).astype(jnp.bfloat16)
        act[i, :, lanes] = result
        return result

    for j in range(count // 2):
        left, right = activate(2 * j, 0, 128), activate(2 * j + 1, 0, 128)
        falling[j] = jnp.where(half, left, turn(right, 64))
        left, right = activate(2 * j, 384, 128), activate(2 * j + 1, 384, 128)
        rising[j] = jnp.where(half, turn(left, 64), right)

    def remote(n, src, dst, other):
        return pltpu.make_async_remote_copy(
            src_ref=src, dst_ref=dst, send_sem=send_sem.at[n], recv_sem=recv_sem.at[n],
            device_id=coords(other), device_id_type=pl.DeviceIdType.MESH,
        )

    rise = remote(0, rising, risen, device + 1)
    fall = remote(1, falling, fallen, device - 1)
    mate = device + 1 - 2 * (device % 2)
    swap_keys = remote(2, keys, keys_in, mate)

    pl.semaphore_wait(barrier, has_left.astype(jnp.int32) + has_right.astype(jnp.int32))

    @pl.when(has_right)
    def _():
        rise.start()

    @pl.when(has_left)
    def _():
        fall.start()

    loads[4].wait()
    keys[...] = jnp.broadcast_to(
        column(map_ref[...].astype(jnp.float32)).astype(jnp.int32), keys.shape
    )
    swap_keys.start()

    for load in loads[5:]:
        load.wait()
    shift = column(shift_ref[...])
    bias = column(bias_ref[...])
    stride_t = flipped(stride[...])
    for a in range(3):
        weight_t[64 * a : 64 * a + 64] = flipped(weight[576 * a : 576 * a + 576])

    for i in range(count):
        activate(i, 128, 256)
    y_low = (lane & 63) < 32
    z_low = (lane & 7) < 4
    marks = ((lane & 63) < 8, (lane & 63) >= 56)

    def row(i, dx, dy, dz):
        target = near_ref[i, offset(dx, dy, dz)]
        local = jnp.clip(target - (device + dx) * count, 0, count - 1)
        return jnp.where(target < 0, count, local)

    def middle(i, carry):
        rows = {
            (dy, dz): row(i, 0, dy, dz)
            for dy in (-1, 0, 1) for dz in (-1, 0, 1) if (dy, dz) != (0, 0)
        }
        columns = []
        for p in range(4):

            def own(dy, dz):
                return act[rows[dy, dz], :, 128 * p : 128 * p + 128]

            tile = act[i, :, 128 * p : 128 * p + 128]
            columns.append((tile, *halos(own, y_low, z_low)))
        product = dot(weight_t[...], stack(columns, marks, side[...]))

        def part(dx, p):
            if not 0 <= p < 4:
                return jnp.zeros((64, 128), jnp.float32)
            return product[64 * (dx + 1) : 64 * (dx + 2), 128 * p : 128 * p + 128]

        pieces = []
        for p in range(4):
            below = jnp.where(half, part(-1, p), part(-1, p - 1))
            above = jnp.where(half, part(1, p + 1), part(1, p))
            pieces.append(part(0, p) + turn(below + above, 64))
        conv[i] = jnp.concatenate(pieces, axis=1)
        return carry

    lax.fori_loop(0, count, middle, 0, unroll=count)

    @pl.when(has_left)
    def _():
        rise.wait_recv()
        fall.wait_send()

    @pl.when(has_right)
    def _():
        fall.wait_recv()
        rise.wait_send()

    for j in range(count // 2):
        lower[2 * j] = turn(risen[j], 64)
        lower[2 * j + 1] = risen[j]
        upper[2 * j] = fallen[j]
        upper[2 * j + 1] = turn(fallen[j], 64)

    outside = jnp.concatenate([weight_t[0:64], weight_t[128:192]], axis=0)
    tall = []
    for i in range(count):

        def outer(dy, dz):
            return jnp.where(half, upper[row(i, 1, dy, dz)], lower[row(i, -1, dy, dz)])

        tall.append((outer(0, 0), *halos(outer, y_low, z_low)))
    stacked = stack(tall, marks, side[...])
    product = dot(outside, stacked)
    for i in range(count):
        mine = product[:, 128 * i : 128 * i + 128]
        turned = pltpu.roll(jnp.where(half, mine[64:], mine[:64]), 64, 1)
        mask = occ_ref[pl.ds(i, 1), :].astype(jnp.float32)
        summed = feat[i].astype(jnp.float32) + conv[i] + shift
        ends = jnp.concatenate(
            [
                jnp.where(half, turned, 0.0),
                jnp.zeros((64, 256), jnp.float32),
                jnp.where(half, 0.0, turned),
            ],
            axis=1,
        )
        fine[i] = (mask * (summed + ends)).astype(jnp.bfloat16)
    ordered = dot(fine[...].reshape(count * 64, 512), perm[...])
    columns = []
    for j in range(0, count, 2):
        taps = []
        for s in range(4):
            one = ordered[64 * j : 64 * j + 64, 128 * s : 128 * s + 128]
            two = ordered[64 * j + 64 : 64 * j + 128, 128 * s : 128 * s + 128]
            taps.append(jnp.where(half, one, pltpu.roll(two, 64, 1)))
            taps.append(jnp.where(half, pltpu.roll(one, 64, 1), two))
        columns.append(jnp.concatenate(taps, axis=0).astype(jnp.bfloat16))
    octants = dot(stride_t, jnp.concatenate(columns, axis=1)) + bias
    octs[...] = octants.astype(jnp.bfloat16)
    swap = remote(3, octs, octs_in, mate)
    swap.start()

    swap_keys.wait()
    swap.wait()


def finish(fine, keys, keys_in, octs, octs_in, fine_hbm, coarse_hbm, coarse, sem):
    count = fine.shape[0]
    device = lax.axis_index("bricks") * lax.axis_size("grp") + lax.axis_index("grp")
    store = pltpu.make_async_copy(fine, fine_hbm, sem.at[0])
    store.start()
    total = place(keys[...], octs[...], device, count)
    total = total + place(keys_in[...], octs_in[...], device, count)
    coarse[0] = total.astype(jnp.bfloat16)
    last = pltpu.make_async_copy(coarse, coarse_hbm, sem.at[1])
    last.start()
    store.wait()
    last.wait()


def shards(
    features, occupancy, neighbours, coarse_map, norm_gain, time_shift, conv_weight,
    stride_weight, coarse_bias,
):
    count = features.shape[0]
    bf16 = jnp.bfloat16
    hbm = pl.BlockSpec(memory_space=pltpu.HBM)
    vmem = pl.BlockSpec(memory_space=pltpu.VMEM)
    found = pl.pallas_call(
        kernel,
        out_shape=(
            jax.ShapeDtypeStruct(features.shape, bf16),
            jax.ShapeDtypeStruct((count, 128), jnp.int32),
            jax.ShapeDtypeStruct((count, 128), jnp.int32),
            jax.ShapeDtypeStruct((128, 64 * count), bf16),
            jax.ShapeDtypeStruct((128, 64 * count), bf16),
        ),
        in_specs=[hbm] * 11,
        out_specs=(vmem,) * 5,
        scratch_shapes=[
            pltpu.VMEM((count, 512), jnp.int32),
            pltpu.VMEM((1, 64), jnp.float32),
            pltpu.VMEM((count, 64, 512), bf16),
            pltpu.VMEM((1, count), jnp.int32),
            pltpu.SMEM((count, 26), jnp.int32),
            pltpu.VMEM((1728, 64), bf16),
            pltpu.VMEM((256, 256), bf16),
            pltpu.VMEM((512, 512), bf16),
            pltpu.VMEM((512, 128), bf16),
            pltpu.VMEM((1, 64), jnp.float32),
            pltpu.VMEM((1, 128), jnp.float32),
            pltpu.VMEM((count + 1, 64, 512), bf16),
            pltpu.VMEM((count + 1, 64, 128), bf16),
            pltpu.VMEM((count + 1, 64, 128), bf16),
            pltpu.VMEM((count, 64, 512), jnp.float32),
            pltpu.VMEM((192, 576), bf16),
            pltpu.VMEM((count // 2, 64, 128), bf16),
            pltpu.VMEM((count // 2, 64, 128), bf16),
            pltpu.VMEM((count // 2, 64, 128), bf16),
            pltpu.VMEM((count // 2, 64, 128), bf16),
            pltpu.SemaphoreType.DMA((16,)),
            pltpu.SemaphoreType.DMA((5,)),
            pltpu.SemaphoreType.DMA((5,)),
        ],
        compiler_params=pltpu.CompilerParams(
            collective_id=0, has_side_effects=True, vmem_limit_bytes=32 * 1024 * 1024
        ),
        name="bricks",
    )(*[
        pltpu.with_memory_space_constraint(x, pltpu.HBM)
        for x in (
            occupancy, norm_gain[None], features, coarse_map[None], neighbours,
            conv_weight.reshape(1728, 64), side_matrix(), stride_matrix(),
            stride_weight.reshape(512, 128), time_shift[None], coarse_bias[None],
        )
    ])
    return pl.pallas_call(
        finish,
        out_shape=(
            jax.ShapeDtypeStruct(features.shape, bf16),
            jax.ShapeDtypeStruct((1, 128, 512), bf16),
        ),
        in_specs=[vmem] * 5,
        out_specs=(hbm, hbm),
        scratch_shapes=[pltpu.VMEM((1, 128, 512), bf16), pltpu.SemaphoreType.DMA((2,))],
        compiler_params=pltpu.CompilerParams(vmem_limit_bytes=16 * 1024 * 1024),
        name="finish",
    )(*found)


def solution(mesh):
    wide = P(AXES, None, None)
    return jax.shard_map(
        shards,
        mesh=mesh,
        in_specs=(wide, P(AXES, None), P(AXES, None), P(AXES), P(), P(), P(), P(), P()),
        out_specs=(wide, wide),
        check_vma=False,
    )
```
